32 devices in a mesh: row: 4 (over y, core), col: 8 (over z, x).
Axes of the slice: x: 2, y: 2, z: 4, core: 2. Of those that a mesh axis runs over, the one named last changes fastest.
Arguments:
- ancestor: bfloat16 [32, 32, 256, 256], P('row', 'col'), may hold values from -6 to 6
- tile_mask: int32 [32, 32], P('row', 'col'), may hold values 0 or 1
- member_one: int32 [32], replicated, may hold values 0 or 1
- member_two: int32 [32], replicated, may hold values 0 or 1
- factor_one: bfloat16 [32, 256, 256], P('row'), may hold values from -0.0625 to 0.0625
- factor_two: bfloat16 [32, 256, 256], P('row'), may hold values from -0.0625 to 0.0625
- link_block: bfloat16 [256, 256], replicated, may hold values from -0.375 to 0.375
- inverse_one: float32 [256, 256], replicated, may hold values from -6 to 6
- inverse_two: float32 [256, 256], replicated, may hold values from -6 to 6
Outputs:
- column_one: bfloat16 [32, 256, 256], P(('row', 'col'))
- column_two: bfloat16 [32, 256, 256], P(('row', 'col'))
- diag_one: bfloat16 [256, 256], replicated
- cross_block: bfloat16 [256, 256], replicated
- diag_two: bfloat16 [256, 256], replicated
The draws below stay inside these ranges and needn't reach their ends.
All inputs are finite; a program needn't handle non-finite values. No bound on the sum of `tile_mask` on one device may be relied on, other than what follows from the above.
Results may differ from the reference program's by a relative error of at most 0.01.
Values may be sent and summed in bfloat16 or wider, within the bound.
No kernel may reach another device: no remote copies, remote signals or barrier semaphores. Data moves between devices by JAX's collectives and lax.ppermute only.
A program may use at most 128 MiB of HBM per device.

```python
import jax
import jax.numpy as jnp
from jax import lax

TILE = 256
TILES = 32


def set_ends(drawn, stream_key, low, high):
    place = [jax.random.randint(jax.random.fold_in(stream_key, axis), (), 0, length) for axis, length in enumerate(drawn.shape)]
    widest = drawn.shape.index(max(drawn.shape))
    beside = place[:widest] + [(place[widest] + 1) % drawn.shape[widest]] + place[widest + 1:]
    return drawn.at[tuple(place)].set(low).at[tuple(beside)].set(high)


def levels(stream_key, shape, shards, least, largest):
    loudness, own = 1.0, jax.random.fold_in(stream_key, 6)
    for axis_at, parts in shards:
        steps = jnp.exp(jax.random.uniform(jax.random.fold_in(own, axis_at), (parts,), jnp.float32, least / len(shards), largest / len(shards)))
        loudness = loudness * jnp.repeat(steps, shape[axis_at] // parts).reshape([-1 if axis == axis_at else 1 for axis in range(len(shape))])
    return loudness


def normal_values(key, dims, deviation, most, shards=(), kind=jnp.bfloat16):
    array = deviation * jax.random.normal(key, dims, jnp.float32)
    if shards:
        array = array * levels(key, dims, shards, -0.22, 0.18)
    return jnp.clip(array, -most, most).astype(kind)


def setup_inputs(seed: int = 0) -> dict:
    streams_of = jax.random.split(jax.random.key(seed), 10)
    ancestor = normal_values(streams_of[0], (TILES, TILES, TILE, TILE), 1.0, 6.0, ((0, 4), (1, 8)))
    tile_mask = set_ends((jax.random.randint(streams_of[1], (TILES, TILES), 0, 5) < 3).astype(jnp.int32), jax.random.fold_in(streams_of[1], 1), 0, 1)
    member_one = set_ends((jax.random.randint(streams_of[2], (TILES,), 0, 4) < 3).astype(jnp.int32), jax.random.fold_in(streams_of[2], 1), 0, 1)
    member_two = set_ends((jax.random.randint(streams_of[3], (TILES,), 0, 4) < 3).astype(jnp.int32), jax.random.fold_in(streams_of[3], 1), 0, 1)
    factor_one = normal_values(streams_of[4], (TILES, TILE, TILE), (TILES * TILE) ** -0.5, 0.0625, ((0, 4),))
    factor_two = normal_values(streams_of[5], (TILES, TILE, TILE), (TILES * TILE) ** -0.5, 0.0625, ((0, 4),))
    link_block = normal_values(streams_of[6], (TILE, TILE), TILE ** -0.5, 0.375)
    inverse_one = normal_values(streams_of[7], (TILE, TILE), 1.0, 6.0, (), jnp.float32)
    inverse_two = normal_values(streams_of[8], (TILE, TILE), 1.0, 6.0, (), jnp.float32)
    return {"ancestor": ancestor, "tile_mask": tile_mask, "member_one": member_one, "member_two": member_two, "factor_one": factor_one, "factor_two": factor_two, "link_block": link_block, "inverse_one": inverse_one, "inverse_two": inverse_two}


def reference(ancestor, tile_mask, member_one, member_two, factor_one, factor_two, link_block, inverse_one, inverse_two):
    hp = lax.Precision.HIGHEST
    zero = jnp.zeros((), jnp.bfloat16)
    first = jnp.where(member_one[:, None, None] > 0, factor_one, zero)
    second = jnp.where(member_two[:, None, None] > 0, factor_two, zero)
    stacked = jnp.stack([first, second], 1).astype(jnp.float32)

    def one_row(item):
        tiles, marks = item
        kept = jnp.where(marks[:, None, None] > 0, tiles, zero).astype(jnp.float32)
        return jnp.einsum('jab,jkbc->kac', kept, stacked, precision=hp)

    products = lax.map(one_row, (ancestor, tile_mask))
    weight_one = member_one.astype(jnp.float32)[:, None, None]
    weight_two = member_two.astype(jnp.float32)[:, None, None]
    first_f = first.astype(jnp.float32)
    second_f = second.astype(jnp.float32)
    link_f = link_block.astype(jnp.float32)
    y_one = weight_one * products[:, 0]
    column_one = (-y_one).astype(jnp.bfloat16)
    diag_one = (inverse_one + jnp.einsum('sab,sac->bc', first_f, y_one, precision=hp)).astype(jnp.bfloat16)
    y_two = weight_two * (products[:, 1] + jnp.einsum('sab,bc->sac', column_one.astype(jnp.float32), link_f, precision=hp))
    column_two = (-y_two).astype(jnp.bfloat16)
    vsum = jnp.einsum('sab,sac->bc', column_one.astype(jnp.float32), second_f, precision=hp)
    cross_block = (-(vsum + jnp.dot(diag_one, link_block, preferred_element_type=jnp.float32))).astype(jnp.bfloat16)
    diag_two = inverse_two + jnp.einsum('sab,sac->bc', second_f, y_two, precision=hp)
    diag_two = (diag_two - jnp.dot(link_block.T, cross_block, preferred_element_type=jnp.float32)).astype(jnp.bfloat16)
    return column_one, column_two, diag_one, cross_block, diag_two
```

```python
import jax
import jax.numpy as jnp
from jax import lax
from jax.sharding import PartitionSpec as P


def shards(
    ancestor,
    tile_mask,
    member_one,
    member_two,
    factor_one,
    factor_two,
    link_block,
    inverse_one,
    inverse_two,
):
    f32, bf16 = jnp.float32, jnp.bfloat16
    nrow, ncol = lax.axis_size("row"), lax.axis_size("col")
    row, col = lax.axis_index("row"), lax.axis_index("col")
    rows, cols = ancestor.shape[0], ancestor.shape[1]
    tile = ancestor.shape[-1]
    both = ("row", "col")
    group = ncol // nrow
    inner = 2
    outer = ncol // inner
    z, x = col // inner, col % inner
    zero = jnp.zeros((), bf16)

    flags_one = lax.dynamic_slice_in_dim(member_one, row * rows, rows, 0)
    flags_two = lax.dynamic_slice_in_dim(member_two, row * rows, rows, 0)
    first = jnp.where(flags_one[:, None, None] > 0, factor_one, zero)
    second = jnp.where(flags_two[:, None, None] > 0, factor_two, zero)

    piece = jnp.stack([first, second])
    piece = lax.dynamic_slice_in_dim(piece, col % group * cols, cols, 1)
    column = piece
    for k in range(1, nrow):
        perm = [(c // group * ncol + c, (c // group + k) % nrow * ncol + c) for c in range(ncol)]
        got = lax.ppermute(piece, both, perm)
        column = jnp.where((row - col // group) % nrow == k, got, column)

    kept = jnp.where(tile_mask[:, :, None, None] > 0, ancestor, zero)
    partial = jnp.einsum("ijab,kjbc->kiac", kept, column, preferred_element_type=f32)
    partial_low = partial.astype(bf16)

    second_in_one = jnp.where(flags_one[:, None, None] > 0, second, zero)
    c_one = jnp.einsum("sab,sac->bc", first, partial_low[0], preferred_element_type=f32)
    c_cross = jnp.einsum("sab,sac->bc", second_in_one, partial_low[0], preferred_element_type=f32)
    c_two = jnp.einsum("sab,sac->bc", second, partial_low[1], preferred_element_type=f32)
    sums = lax.psum(jnp.stack([c_one, c_cross, c_two]).astype(bf16), both).astype(f32)
    sum_one, sum_cross, sum_two = sums[0], sums[1], sums[2]

    split = partial_low.reshape(2, outer, inner, tile, tile)
    away = lax.dynamic_slice_in_dim(split, (x + 1) % inner, 1, 2)[:, :, 0]
    mine = lax.dynamic_slice_in_dim(split, x, 1, 2)[:, :, 0]
    perm = [
        (r * ncol + c, r * ncol + c // inner * inner + (c + 1) % inner)
        for r in range(nrow)
        for c in range(ncol)
    ]
    got = lax.ppermute(away, both, perm)
    half = (mine.astype(f32) + got.astype(f32)).astype(bf16)
    total = lax.dynamic_slice_in_dim(half, z, 1, 1)[:, 0].astype(f32)
    for k in range(1, outer):
        send = lax.dynamic_slice_in_dim(half, (z + k) % outer, 1, 1)[:, 0]
        perm = [
            (r * ncol + c, r * ncol + (c // inner + k) % outer * inner + c % inner)
            for r in range(nrow)
            for c in range(ncol)
        ]
        total = total + lax.ppermute(send, both, perm).astype(f32)

    mine_one = lax.dynamic_index_in_dim(flags_one, col, keepdims=False).astype(f32)
    mine_two = lax.dynamic_index_in_dim(flags_two, col, keepdims=False).astype(f32)
    column_one = (-mine_one * total[0]).astype(bf16)
    y_two = mine_two * (total[1] + jnp.dot(column_one, link_block, preferred_element_type=f32))
    column_two = (-y_two).astype(bf16)

    diag_one = (inverse_one + sum_one).astype(bf16)
    cross_block = (
        sum_cross.T - jnp.dot(diag_one, link_block, preferred_element_type=f32)
    ).astype(bf16)
    diag_two = (
        inverse_two
        + sum_two
        - jnp.dot(sum_cross.astype(bf16), link_block, preferred_element_type=f32)
        - jnp.dot(link_block.T, cross_block, preferred_element_type=f32)
    ).astype(bf16)
    return (column_one[None], column_two[None], diag_one, cross_block, diag_two)


def solution(mesh):
    in_specs = (
        P("row", "col", None, None),
        P("row", "col"),
        P(),
        P(),
        P("row", None, None),
        P("row", None, None),
        P(),
        P(),
        P(),
    )
    out_specs = (P(("row", "col"), None, None), P(("row", "col"), None, None), P(), P(), P())
    return jax.shard_map(shards, mesh=mesh, in_specs=in_specs, out_specs=out_specs, check_vma=False)
```

```python
import functools

import jax
import jax.numpy as jnp
from jax import lax
from jax.experimental import pallas as pl
from jax.experimental.pallas import tpu as pltpu
from jax.sharding import PartitionSpec as P

F32, BF16 = jnp.float32, jnp.bfloat16
BOTH = ("row", "col")


def product_kernel(cols, n_fac, ids, marks, flags, *refs):
    anc, column = refs[:2]
    factors, (out, sums), acc = refs[2 : 2 + n_fac], refs[2 + n_fac : 4 + n_fac], refs[-1]
    step = pl.program_id(0)
    s = ids[step]

    @pl.when(step == 0)
    def _():
        sums[...] = jnp.zeros_like(sums)

    acc[...] = jnp.zeros_like(acc)
    for j in range(cols):

        @pl.when(marks[s * cols + j] > 0)
        def _(j=j):
            acc[...] += jnp.dot(anc[0, j], column[j], preferred_element_type=F32)

    low = acc[...].astype(BF16)
    out[0] = low
    for k in range(n_fac):

        @pl.when(flags[s * n_fac + k] > 0)
        def _(k=k):
            sums[k] += lax.dot_general(
                factors[k][0], low, (((0,), (0,)), ((), ())), preferred_element_type=F32
            )


def products(ids, marks, flags, ancestor, column, factors):
    rows, cols, tile, _ = ancestor.shape
    n, n_fac = ids.shape[0], len(factors)
    block = lambda i, ids, *_: (ids[i], 0, 0)
    return pl.pallas_call(
        functools.partial(product_kernel, cols, n_fac),
        out_shape=(
            jax.ShapeDtypeStruct((n, tile, tile), BF16),
            jax.ShapeDtypeStruct((n_fac, tile, tile), F32),
        ),
        grid_spec=pltpu.PrefetchScalarGridSpec(
            num_scalar_prefetch=3,
            grid=(n,),
            in_specs=[
                pl.BlockSpec((1, cols, tile, tile), lambda i, ids, *_: (ids[i], 0, 0, 0)),
                pl.BlockSpec((cols, tile, tile), lambda i, *_: (0, 0, 0)),
            ]
            + [pl.BlockSpec((1, tile, tile), block)] * n_fac,
            out_specs=[
                pl.BlockSpec((1, tile, tile), lambda i, *_: (i, 0, 0)),
                pl.BlockSpec((n_fac, tile, tile), lambda i, *_: (0, 0, 0)),
            ],
            scratch_shapes=[pltpu.VMEM((tile, tile), F32)],
        ),
        compiler_params=pltpu.CompilerParams(vmem_limit_bytes=32 << 20),
        cost_estimate=pl.CostEstimate(
            flops=2 * n * (cols + n_fac) * tile**3,
            bytes_accessed=2 * n * (cols + n_fac + 1) * tile**2,
            transcendentals=0,
        ),
    )(ids, marks, flags, ancestor, column, *factors)


def shards(
    ancestor,
    tile_mask,
    member_one,
    member_two,
    factor_one,
    factor_two,
    link_block,
    inverse_one,
    inverse_two,
):
    nrow, ncol = lax.axis_size("row"), lax.axis_size("col")
    row, col = lax.axis_index("row"), lax.axis_index("col")
    rows, cols, tile = ancestor.shape[0], ancestor.shape[1], ancestor.shape[-1]
    group = ncol // nrow
    bits = ncol.bit_length() - 1
    owner = col // group
    at = lambda r, c: r * ncol + c

    def spread(factor):
        have = piece = lax.dynamic_slice_in_dim(factor, col % group * cols, cols, 0)
        for k in range(2, nrow, 2):
            perm = [(at(c // group, c), at((c // group + k) % nrow, c)) for c in range(ncol)]
            have = jnp.where((row - owner) % nrow == k, lax.ppermute(piece, BOTH, perm), have)
        perm = [
            (at(2 * y + c // group % 2, c), at(2 * y + 1 - c // group % 2, c))
            for y in range(nrow // 2)
            for c in range(ncol)
        ]
        return jnp.where((row - owner) % 2 == 0, have, lax.ppermute(have, BOTH, perm))

    def halves(array, bit):
        split = array.reshape(array.shape[0] // 2, 2, tile, tile)
        mine = (col >> bit) & 1
        pick = lambda b: lax.dynamic_slice_in_dim(split, b, 1, 1)[:, 0]
        return pick(1 - mine), pick(mine)

    def swap(array, bit):
        perm = [(at(r, c), at(r, c ^ (1 << bit))) for r in range(nrow) for c in range(ncol)]
        return lax.ppermute(array, BOTH, perm)

    flags_one = lax.dynamic_slice_in_dim(member_one, row * rows, rows, 0)
    flags_two = lax.dynamic_slice_in_dim(member_two, row * rows, rows, 0)
    marks = [
        (tile_mask * lax.dynamic_slice_in_dim(m, col * cols, cols, 0)[None]).reshape(-1)
        for m in (member_one, member_two)
    ]
    flags = [jnp.stack([flags_one, flags_one * flags_two], 1).reshape(-1), flags_two]
    ids = jnp.arange(rows // 2, dtype=jnp.int32) * 2
    leave, stay = ids + (1 - col % 2), ids + col % 2

    totals, contracted = [], []
    factors = [(factor_one, factor_two), (factor_two,)]
    for k, factor in enumerate((factor_one, factor_two)):
        column = spread(factor)
        args = (marks[k], flags[k], ancestor, column, factors[k])
        away, part_a = products(leave, *args)
        got = swap(away, 0)
        keep, part_b = products(stay, *args)
        contracted.append(part_a + part_b)
        for bit in range(1, bits):
            summed = keep.astype(F32) + got.astype(F32)
            away, keep = halves(summed, bit)
            got = swap(away.astype(BF16), bit)
        totals.append((keep.astype(F32) + got.astype(F32))[0])

    parts = jnp.concatenate(contracted).astype(BF16)
    high = parts.shape[0] * tile // nrow
    part = lax.all_to_all(parts.reshape(nrow, high, tile), "row", 0, 0)
    part = part.astype(F32).sum(0).astype(BF16)
    part = lax.all_to_all(part.reshape(ncol, high // ncol, tile), "col", 0, 0)
    part = part.astype(F32).sum(0).astype(BF16)
    part = lax.all_to_all(jnp.broadcast_to(part, (ncol,) + part.shape), "col", 0, 0)
    part = part.reshape(high, tile)
    part = lax.all_to_all(jnp.broadcast_to(part, (nrow,) + part.shape), "row", 0, 0)
    sum_one, sum_cross, sum_two = part.reshape(parts.shape)

    mine_one = lax.dynamic_index_in_dim(flags_one, col, keepdims=False).astype(F32)
    mine_two = lax.dynamic_index_in_dim(flags_two, col, keepdims=False).astype(F32)
    column_one = (-mine_one * totals[0]).astype(BF16)
    y_two = mine_two * (totals[1] + jnp.dot(column_one, link_block, preferred_element_type=F32))
    column_two = (-y_two).astype(BF16)

    diag_one = (inverse_one + sum_one.astype(F32)).astype(BF16)
    cross_block = (
        sum_cross.astype(F32).T - jnp.dot(diag_one, link_block, preferred_element_type=F32)
    ).astype(BF16)
    diag_two = (
        inverse_two
        + sum_two.astype(F32)
        - jnp.dot(sum_cross, link_block, preferred_element_type=F32)
        - jnp.dot(link_block.T, cross_block, preferred_element_type=F32)
    ).astype(BF16)
    return (column_one[None], column_two[None], diag_one, cross_block, diag_two)


def solution(mesh):
    in_specs = (
        P("row", "col", None, None),
        P("row", "col"),
        P(),
        P(),
        P("row", None, None),
        P("row", None, None),
        P(),
        P(),
        P(),
    )
    out_specs = (P(("row", "col"), None, None), P(("row", "col"), None, None), P(), P(), P())
    return jax.shard_map(shards, mesh=mesh, in_specs=in_specs, out_specs=out_specs, check_vma=False)
```

```python
import functools

import jax
import jax.numpy as jnp
from jax import lax
from jax.experimental import pallas as pl
from jax.experimental.pallas import tpu as pltpu
from jax.sharding import PartitionSpec as P

F32, BF16 = jnp.float32, jnp.bfloat16
BOTH = ("row", "col")


def transposed_dot(a, b):
    return lax.dot_general(a, b, (((0,), (0,)), ((), ())), preferred_element_type=F32)


def column_kernel(members, keep_one, got_one, keep_two, got_two, link, column_one, column_two):
    member = [members[k].astype(F32) for k in range(2)]
    one = -member[0] * (keep_one[...].astype(F32) + got_one[...].astype(F32))
    column_one[...] = one.astype(BF16)
    two = keep_two[...].astype(F32) + got_two[...].astype(F32)
    two += jnp.dot(column_one[...], link[...], preferred_element_type=F32)
    column_two[...] = (-member[1] * two).astype(BF16)


def diagonal_kernel(sums, link, inverse_one, inverse_two, diag_one, cross, diag_two):
    diag_one[...] = (inverse_one[...] + sums[0].astype(F32)).astype(BF16)
    step = jnp.dot(diag_one[...], link[...], preferred_element_type=F32)
    cross[...] = (sums[1].astype(F32) - step).astype(BF16)
    two = inverse_two[...] + sums[2].astype(F32) - transposed_dot(sums[1], link[...])
    diag_two[...] = (two - transposed_dot(link[...], cross[...])).astype(BF16)


def small_kernel(body, n_out, n_dots, tile, operands, scalars=0):
    memory = [pltpu.SMEM] * scalars + [pltpu.VMEM] * (len(operands) - scalars)
    return pl.pallas_call(
        body,
        out_shape=(jax.ShapeDtypeStruct((tile, tile), BF16),) * n_out,
        in_specs=[pl.BlockSpec(memory_space=space) for space in memory],
        out_specs=[pl.BlockSpec(memory_space=pltpu.VMEM)] * n_out,
        cost_estimate=pl.CostEstimate(
            flops=2 * n_dots * tile**3,
            bytes_accessed=4 * len(operands) * tile**2,
            transcendentals=0,
        ),
    )(*operands)


def product_kernel(cols, n_fac, ids, marks, flags, *refs):
    anc, column = refs[:2]
    factors, (away, keep, sums, acc) = refs[2 : 2 + n_fac], refs[2 + n_fac :]
    step, half = pl.program_id(0), pl.num_programs(0) // 2
    s = ids[step]

    @pl.when(step == 0)
    def _():
        sums[...] = jnp.zeros_like(sums)

    acc[...] = jnp.zeros_like(acc)
    for j in range(cols):

        @pl.when(marks[s * cols + j] > 0)
        def _(j=j):
            acc[...] += jnp.dot(anc[0, j], column[j], preferred_element_type=F32)

    low = acc[...].astype(BF16)

    @pl.when(step < half)
    def _():
        away[0] = low

    @pl.when(step >= half)
    def _():
        keep[0] = low

    for k in range(n_fac):

        @pl.when(flags[s * n_fac + k] > 0)
        def _(k=k):
            pair = (low, factors[k][0]) if k else (factors[k][0], low)
            sums[k] += transposed_dot(*pair)


def products(ids, marks, flags, ancestor, column, factors):
    rows, cols, tile, _ = ancestor.shape
    n, n_fac = ids.shape[0], len(factors)
    block = lambda i, ids, *_: (ids[i], 0, 0)
    return pl.pallas_call(
        functools.partial(product_kernel, cols, n_fac),
        out_shape=(
            jax.ShapeDtypeStruct((n // 2, tile, tile), BF16),
            jax.ShapeDtypeStruct((n // 2, tile, tile), BF16),
            jax.ShapeDtypeStruct((n_fac, tile, tile), F32),
        ),
        grid_spec=pltpu.PrefetchScalarGridSpec(
            num_scalar_prefetch=3,
            grid=(n,),
            in_specs=[
                pl.BlockSpec((1, cols, tile, tile), lambda i, ids, *_: (ids[i], 0, 0, 0)),
                pl.BlockSpec((cols, tile, tile), lambda i, *_: (0, 0, 0)),
            ]
            + [pl.BlockSpec((1, tile, tile), block)] * n_fac,
            out_specs=[
                pl.BlockSpec((1, tile, tile), lambda i, *_: (jnp.minimum(i, n // 2 - 1), 0, 0)),
                pl.BlockSpec((1, tile, tile), lambda i, *_: (jnp.maximum(i - n // 2, 0), 0, 0)),
                pl.BlockSpec((n_fac, tile, tile), lambda i, *_: (0, 0, 0)),
            ],
            scratch_shapes=[pltpu.VMEM((tile, tile), F32)],
        ),
        compiler_params=pltpu.CompilerParams(vmem_limit_bytes=32 << 20),
        cost_estimate=pl.CostEstimate(
            flops=2 * n * (cols + n_fac) * tile**3,
            bytes_accessed=2 * n * (cols + n_fac + 1) * tile**2,
            transcendentals=0,
        ),
    )(ids, marks, flags, ancestor, column, *factors)


def shards(
    ancestor,
    tile_mask,
    member_one,
    member_two,
    factor_one,
    factor_two,
    link_block,
    inverse_one,
    inverse_two,
):
    nrow, ncol = lax.axis_size("row"), lax.axis_size("col")
    row, col = lax.axis_index("row"), lax.axis_index("col")
    rows, cols, tile = ancestor.shape[0], ancestor.shape[1], ancestor.shape[-1]
    group = ncol // nrow
    bits = ncol.bit_length() - 1
    owner = col // group
    at = lambda r, c: r * ncol + c

    def spread(factor):
        have = piece = lax.dynamic_slice_in_dim(factor, col % group * cols, cols, 0)
        for k in range(2, nrow, 2):
            perm = [(at(c // group, c), at((c // group + k) % nrow, c)) for c in range(ncol)]
            have = jnp.where((row - owner) % nrow == k, lax.ppermute(piece, BOTH, perm), have)
        perm = [
            (at(2 * y + c // group % 2, c), at(2 * y + 1 - c // group % 2, c))
            for y in range(nrow // 2)
            for c in range(ncol)
        ]
        return jnp.where((row - owner) % 2 == 0, have, lax.ppermute(have, BOTH, perm))

    def pick(array, bit, other):
        split = array.reshape(array.shape[0] // 2, 2, tile, tile)
        return lax.dynamic_slice_in_dim(split, (col >> bit & 1) ^ other, 1, 1)[:, 0].astype(F32)

    def swap(array, bit):
        perm = [(at(r, c), at(r, c ^ (1 << bit))) for r in range(nrow) for c in range(ncol)]
        return lax.ppermute(array, BOTH, perm)

    def swap_rows(array, bit):
        perm = [(at(r, c), at(r ^ (1 << bit), c)) for r in range(nrow) for c in range(ncol)]
        return lax.ppermute(array, BOTH, perm)

    flags_one = lax.dynamic_slice_in_dim(member_one, row * rows, rows, 0)
    flags_two = lax.dynamic_slice_in_dim(member_two, row * rows, rows, 0)
    marks = [
        (tile_mask * lax.dynamic_slice_in_dim(m, col * cols, cols, 0)[None]).reshape(-1)
        for m in (member_one, member_two)
    ]
    flags = [jnp.stack([flags_one, flags_one * flags_two], 1).reshape(-1), flags_two]
    ids = jnp.arange(rows // 2, dtype=jnp.int32) * 2
    ids = jnp.concatenate([ids + (1 - col % 2), ids + col % 2])

    totals, contracted, arrived = [], [], []
    factors = [(factor_one, factor_two), (factor_two,)]
    for k, factor in enumerate((factor_one, factor_two)):
        column = spread(factor)
        away, keep, part = products(ids, marks[k], flags[k], ancestor, column, factors[k])
        contracted.append(part)
        got = swap(away, 0)
        arrived.append([got])
        for bit in range(1, bits):
            away = (pick(keep, bit, 1) + pick(got, bit, 1)).astype(BF16)
            keep = pick(keep, bit, 0) + pick(got, bit, 0)
            got = swap(away, bit)
            arrived[k].append(got)
        totals += [keep[0], got[0]]

    parts = jnp.concatenate(contracted)
    shape = parts.shape
    part = parts.reshape(-1, tile)
    row_bits = range(nrow.bit_length() - 1)
    for bit in row_bits:
        half = part.shape[0] // 2
        if bit == 1:
            part, _ = lax.optimization_barrier((part, arrived[0][0]))
        mine = row >> bit & 1
        got = swap_rows(lax.dynamic_slice_in_dim(part, (1 - mine) * half, half, 0).astype(BF16), bit)
        part = lax.dynamic_slice_in_dim(part, mine * half, half, 0) + got.astype(F32)
    part = part.astype(BF16)
    after = [None] + [arrived[0][1]] * (bits - 2) + [arrived[1][0]]
    for bit in range(bits):
        if bit:
            part, _ = lax.optimization_barrier((part, after[bit]))
        part = (part.astype(F32) + swap(part, bit).astype(F32)).astype(BF16)
    for bit in reversed(row_bits):
        part, _ = lax.optimization_barrier((part, arrived[1][1] if bit == 0 else arrived[0][-1]))
        got = swap_rows(part, bit)
        low = (row >> bit & 1) == 0
        part = jnp.concatenate([jnp.where(low, part, got), jnp.where(low, got, part)])

    members = jnp.stack([lax.dynamic_index_in_dim(m, col, keepdims=False) for m in (flags_one, flags_two)])
    column_one, column_two = small_kernel(
        column_kernel, 2, 1, tile, (members, *totals, link_block), 1
    )
    diag_one, cross_block, diag_two = small_kernel(
        diagonal_kernel, 3, 3, tile, (part.reshape(shape), link_block, inverse_one, inverse_two)
    )
    return (column_one[None], column_two[None], diag_one, cross_block, diag_two)


def solution(mesh):
    in_specs = (
        P("row", "col", None, None),
        P("row", "col"),
        P(),
        P(),
        P("row", None, None),
        P("row", None, None),
        P(),
        P(),
        P(),
    )
    out_specs = (P(("row", "col"), None, None), P(("row", "col"), None, None), P(), P(), P())
    return jax.shard_map(shards, mesh=mesh, in_specs=in_specs, out_specs=out_specs, check_vma=False)
```

```python
import functools

import jax
import jax.numpy as jnp
from jax import lax
from jax.experimental import pallas as pl
from jax.experimental.pallas import tpu as pltpu
from jax.sharding import PartitionSpec as P

F32, BF16 = jnp.float32, jnp.bfloat16
BOTH = ("row", "col")


def transposed_dot(a, b):
    return lax.dot_general(a, b, (((0,), (0,)), ((), ())), preferred_element_type=F32)


def wide(ref, k):
    return jnp.concatenate([ref[2 * k], ref[2 * k + 1]], axis=-1)


def column_kernel(first, second, place, link, *refs):
    (keep_one, got_one), halves, (column_one, column_two) = refs[:2], refs[2:-2], refs[-2:]
    member_one, member_two = (m[place[0]].astype(F32) for m in (first, second))
    one = keep_one[...].astype(F32) + got_one[...].astype(F32)
    column_one[...] = (-member_one * one).astype(BF16)
    two = [halves[2 * k][...].astype(F32) + halves[2 * k + 1][...].astype(F32) for k in range(2)]
    two = jnp.concatenate(two, axis=-1)
    two += jnp.dot(column_one[...], link[...], preferred_element_type=F32)
    column_two[...] = (-member_two * two).astype(BF16)


def diagonal_kernel(sums, link, inverse_one, inverse_two, diag_one, cross, diag_two):
    diag_one[...] = (inverse_one[...] + wide(sums, 0).astype(F32)).astype(BF16)
    step = jnp.dot(diag_one[...], link[...], preferred_element_type=F32)
    crossed = wide(sums, 1)
    cross[...] = (crossed.astype(F32) - step).astype(BF16)
    two = inverse_two[...] + wide(sums, 2).astype(F32) - transposed_dot(crossed, link[...])
    diag_two[...] = (two - transposed_dot(link[...], cross[...])).astype(BF16)


def small_kernel(body, n_out, n_dots, tile, operands, scalars=0):
    memory = [pltpu.SMEM] * scalars + [pltpu.VMEM] * (len(operands) - scalars)
    return pl.pallas_call(
        body,
        out_shape=(jax.ShapeDtypeStruct((tile, tile), BF16),) * n_out,
        in_specs=[pl.BlockSpec(memory_space=space) for space in memory],
        out_specs=[pl.BlockSpec(memory_space=pltpu.VMEM)] * n_out,
        cost_estimate=pl.CostEstimate(
            flops=2 * n_dots * tile**3,
            bytes_accessed=4 * len(operands) * tile**2,
            transcendentals=0,
        ),
    )(*operands)


def product_kernel(n_fac, pieces, ids, marks, flags, anc, column, *refs):
    factors, outs = refs[:n_fac], refs[n_fac:-3]
    sums, tiles, sems = refs[-3:]
    n, cols, tile, _ = tiles.shape
    half, width = n // 2, tile // pieces
    fetch = lambda i: pltpu.make_async_copy(anc.at[ids[i]], tiles.at[i], sems.at[i])
    for i in range(n):
        fetch(i).start()
    sums[...] = jnp.zeros_like(sums)
    zero = jnp.zeros((tile, tile), BF16)
    weights = column[...].reshape(cols * tile, tile)

    def step(i, _, outs):
        s = ids[i]
        fetch(i).wait()
        kept = [jnp.where(marks[s * cols + j] > 0, tiles[i, j], zero) for j in range(cols)]
        low = jnp.dot(
            jnp.concatenate(kept, axis=1), weights, preferred_element_type=F32
        ).astype(BF16)
        for p in range(pieces):
            outs[p][i % half] = low[:, p * width : (p + 1) * width]
        for k in range(n_fac):
            factor = jnp.where(flags[s * n_fac + k] > 0, factors[k][s], zero)
            added = transposed_dot(*((low, factor) if k else (factor, low)))
            sums[2 * k] += added[:, : tile // 2]
            sums[2 * k + 1] += added[:, tile // 2 :]

    lax.fori_loop(0, half, functools.partial(step, outs=outs[:pieces]), None)
    lax.fori_loop(half, n, functools.partial(step, outs=outs[pieces:]), None)


def products(pieces, ids, marks, flags, ancestor, column, factors):
    n, cols, tile, _ = ancestor.shape
    n_fac = len(factors)
    out = jax.ShapeDtypeStruct((n // 2, tile, tile // pieces), BF16)
    shapes = (out,) * (2 * pieces) + (jax.ShapeDtypeStruct((2 * n_fac, tile, tile // 2), F32),)
    memory = [pltpu.SMEM] * 3 + [pltpu.HBM] + [pltpu.VMEM] * (1 + n_fac)
    *outs, sums = pl.pallas_call(
        functools.partial(product_kernel, n_fac, pieces),
        out_shape=shapes,
        in_specs=[pl.BlockSpec(memory_space=space) for space in memory],
        out_specs=[pl.BlockSpec(memory_space=pltpu.VMEM)] * len(shapes),
        scratch_shapes=[
            pltpu.VMEM((n, cols, tile, tile), BF16),
            pltpu.SemaphoreType.DMA((n,)),
        ],
        compiler_params=pltpu.CompilerParams(vmem_limit_bytes=40 << 20),
        cost_estimate=pl.CostEstimate(
            flops=2 * n * (cols + n_fac) * tile**3,
            bytes_accessed=2 * n * (cols + n_fac + 1) * tile**2,
            transcendentals=0,
        ),
    )(ids, marks, flags, ancestor, column, *factors)
    return outs[:pieces], outs[pieces:], sums


def after(array, *earlier):
    return lax.optimization_barrier((array, *earlier))[0]


def shards(
    ancestor,
    tile_mask,
    member_one,
    member_two,
    factor_one,
    factor_two,
    link_block,
    inverse_one,
    inverse_two,
):
    nrow, ncol = lax.axis_size("row"), lax.axis_size("col")
    row, col = lax.axis_index("row"), lax.axis_index("col")
    rows, cols, tile = ancestor.shape[0], ancestor.shape[1], ancestor.shape[-1]
    group = ncol // nrow
    bits, row_bits = ncol.bit_length() - 1, nrow.bit_length() - 1
    owner = col // group
    at = lambda r, c: r * ncol + c
    everyone = [(r, c) for r in range(nrow) for c in range(ncol)]

    def over_chips(factor, *earlier):
        have = piece = lax.dynamic_slice_in_dim(factor, col % group * cols, cols, 0)
        for k in range(2, nrow, 2):
            perm = [(at(c // group, c), at((c // group + k) % nrow, c)) for c in range(ncol)]
            got = after(lax.ppermute(piece, BOTH, perm), *earlier)
            have = jnp.where((row - owner) % nrow == k, got, have)
        return have

    def over_cores(have):
        perm = [
            (at(2 * y + c // group % 2, c), at(2 * y + 1 - c // group % 2, c))
            for y in range(nrow // 2)
            for c in range(ncol)
        ]
        return jnp.where((row - owner) % 2 == 0, have, lax.ppermute(have, BOTH, perm))

    def swap(array, bit):
        return lax.ppermute(array, BOTH, [(at(r, c), at(r, c ^ (1 << bit))) for r, c in everyone])

    def swap_rows(array, bit):
        return lax.ppermute(array, BOTH, [(at(r, c), at(r ^ (1 << bit), c)) for r, c in everyone])

    def pick(array, bit, other):
        split = array.reshape(array.shape[0] // 2, 2, *array.shape[1:])
        return lax.dynamic_slice_in_dim(split, (col >> bit & 1) ^ other, 1, 1)[:, 0].astype(F32)

    def merged(keep, got, bit, other):
        return pick(keep, bit, other) + pick(got, bit, other)

    flags_one = lax.dynamic_slice_in_dim(member_one, row * rows, rows, 0)
    flags_two = lax.dynamic_slice_in_dim(member_two, row * rows, rows, 0)
    marks = [
        (tile_mask * lax.dynamic_slice_in_dim(m, col * cols, cols, 0)[None]).reshape(-1)
        for m in (member_one, member_two)
    ]
    flags = [jnp.stack([flags_one, flags_one * flags_two], 1).reshape(-1), flags_two]
    ids = jnp.arange(rows // 2, dtype=jnp.int32) * 2
    ids = jnp.concatenate([ids + (1 - col % 2), ids + col % 2])

    column = over_cores(over_chips(factor_one, *marks, *flags, ids))
    (away,), (keep_one,), sums_one = products(
        1, ids, marks[0], flags[0], ancestor, column, (factor_one, factor_two)
    )
    one = [swap(away, 0)]
    column = over_cores(over_chips(factor_two, keep_one))
    (away_a, away_b), (keep_a, keep_b), sums_two = products(
        2, ids, marks[1], flags[1], ancestor, column, (factor_two,)
    )

    sums = jnp.concatenate([sums_one, sums_two])
    shape = sums.shape
    part = sums.reshape(-1, shape[-1])
    for bit in range(row_bits):
        half = part.shape[0] // 2
        mine = row >> bit & 1
        if bit == row_bits - 1:
            part = after(part, one[0])
        got = swap_rows(lax.dynamic_slice_in_dim(part, (1 - mine) * half, half, 0).astype(BF16), bit)
        part = lax.dynamic_slice_in_dim(part, mine * half, half, 0) + got.astype(F32)
    part = part.astype(BF16)

    b = []
    for bit in range(bits):
        if bit:
            away = merged(keep_one, one[-1], bit, 1).astype(BF16)
            keep_one = merged(keep_one, one[-1], bit, 0)
            one.append(swap(after(away, b[bit - 2]) if bit > 1 else away, bit))
            away_a = merged(keep_a, got_a, bit, 1).astype(BF16)
            keep_a = merged(keep_a, got_a, bit, 0)
            away_b = merged(keep_b, b[-1], bit, 1).astype(BF16)
            keep_b = merged(keep_b, b[-1], bit, 0)
        else:
            away_b = after(away_b, one[0])
        message = jnp.concatenate([away_a.reshape(-1, tile // 2), part])
        message = swap(after(message, one[bit]), bit)
        b.append(swap(away_b, bit))
        got_a = message[: -part.shape[0]].reshape(away_a.shape)
        part = (part.astype(F32) + message[-part.shape[0] :].astype(F32)).astype(BF16)

    for bit in reversed(range(row_bits)):
        got = swap_rows(after(part, b[-1] if bit == 0 else b[-2]), bit)
        low = (row >> bit & 1) == 0
        part = jnp.concatenate([jnp.where(low, part, got), jnp.where(low, got, part)])

    column_one, column_two = small_kernel(
        column_kernel,
        2,
        1,
        tile,
        (
            member_one,
            member_two,
            (row * rows + col)[None],
            link_block,
            *(a[0] for a in (keep_one, one[-1], keep_a, got_a, keep_b, b[-1])),
        ),
        3,
    )
    diag_one, cross_block, diag_two = small_kernel(
        diagonal_kernel, 3, 3, tile, (part.reshape(shape), link_block, inverse_one, inverse_two)
    )
    return (column_one[None], column_two[None], diag_one, cross_block, diag_two)


def solution(mesh):
    in_specs = (
        P("row", "col", None, None),
        P("row", "col"),
        P(),
        P(),
        P("row", None, None),
        P("row", None, None),
        P(),
        P(),
        P(),
    )
    out_specs = (P(("row", "col"), None, None), P(("row", "col"), None, None), P(), P(), P())
    return jax.shard_map(shards, mesh=mesh, in_specs=in_specs, out_specs=out_specs, check_vma=False)
```

```python
import functools

import jax
import jax.numpy as jnp
from jax import lax
from jax.experimental import pallas as pl
from jax.experimental.pallas import tpu as pltpu
from jax.sharding import PartitionSpec as P

F32, BF16 = jnp.float32, jnp.bfloat16
BOTH = ("row", "col")


def transposed_dot(a, b):
    return lax.dot_general(a, b, (((0,), (0,)), ((), ())), preferred_element_type=F32)


def column_kernel(first, second, place, link, keep_one, got_one, keep_two, got_two, column_one, column_two):
    member_one, member_two = (m[place[0]].astype(F32) for m in (first, second))
    one = keep_one[...].astype(F32) + got_one[...].astype(F32)
    column_one[...] = (-member_one * one).astype(BF16)
    two = keep_two[...].astype(F32) + got_two[...].astype(F32)
    two += jnp.dot(column_one[...], link[...], preferred_element_type=F32)
    column_two[...] = (-member_two * two).astype(BF16)


def diagonal_kernel(sums, link, inverse_one, inverse_two, diag_one, cross, diag_two):
    diag_one[...] = (inverse_one[...] + sums[0].astype(F32)).astype(BF16)
    step = jnp.dot(diag_one[...], link[...], preferred_element_type=F32)
    cross[...] = (sums[1].astype(F32).T - step).astype(BF16)
    two = inverse_two[...] + sums[2].astype(F32)
    two -= jnp.dot(sums[1], link[...], preferred_element_type=F32)
    diag_two[...] = (two - transposed_dot(link[...], cross[...])).astype(BF16)


def small_kernel(body, n_out, n_dots, tile, operands, scalars=0):
    memory = [pltpu.SMEM] * scalars + [pltpu.VMEM] * (len(operands) - scalars)
    return pl.pallas_call(
        body,
        out_shape=(jax.ShapeDtypeStruct((tile, tile), BF16),) * n_out,
        in_specs=[pl.BlockSpec(memory_space=space) for space in memory],
        out_specs=[pl.BlockSpec(memory_space=pltpu.VMEM)] * n_out,
        cost_estimate=pl.CostEstimate(
            flops=2 * n_dots * tile**3,
            bytes_accessed=4 * len(operands) * tile**2,
            transcendentals=0,
        ),
    )(*operands)


def piece_kernel(place, one, two, piece_one, piece_two, sems):
    cols = piece_one.shape[0]
    copies = [
        pltpu.make_async_copy(src.at[pl.ds(place[0], cols)], dst, sems.at[k])
        for k, (src, dst) in enumerate(((one, piece_one), (two, piece_two)))
    ]
    for copy in copies:
        copy.start()
    for copy in copies:
        copy.wait()


def pieces(place, one, two, cols):
    anywhere = pl.BlockSpec(memory_space=pl.ANY)
    return pl.pallas_call(
        piece_kernel,
        out_shape=(jax.ShapeDtypeStruct((cols,) + one.shape[1:], BF16),) * 2,
        in_specs=[pl.BlockSpec(memory_space=pltpu.SMEM), anywhere, anywhere],
        out_specs=[anywhere] * 2,
        scratch_shapes=[pltpu.SemaphoreType.DMA((2,))],
        cost_estimate=pl.CostEstimate(flops=0, bytes_accessed=4 * one.nbytes, transcendentals=0),
    )(place, one, two)


def product_kernel(n_fac, ids, marks, flags, anc, column, *refs):
    factors, outs = refs[:n_fac], refs[n_fac : n_fac + 2]
    sums, tiles, low, sems, out_sems = refs[n_fac + 2 :]
    n, cols, tile, _ = tiles.shape
    half = n // 2
    fetch = lambda i: pltpu.make_async_copy(anc.at[ids[i]], tiles.at[i], sems.at[i])
    leave = lambda h: pltpu.make_async_copy(low.at[pl.ds(h * half, half)], outs[h], out_sems.at[h])
    for i in range(n):
        fetch(i).start()
    zero = jnp.zeros((tile, tile), BF16)
    weights = column[...].reshape(cols * tile, tile)
    for h in range(2):
        block, turned = [], []
        for i in range(h * half, (h + 1) * half):
            fetch(i).wait()
            s = ids[i]
            kept = [jnp.where(marks[s * cols + j] > 0, tiles[i, j], zero) for j in range(cols)]
            block.append(jnp.concatenate(kept, axis=1))
            kept = [jnp.where(flags[s * n_fac + k] > 0, factors[k][s], zero) for k in range(n_fac)]
            turned.append(jnp.concatenate(kept, axis=1))
        product = jnp.dot(
            jnp.concatenate(block, axis=0), weights, preferred_element_type=F32
        ).astype(BF16)
        low[h * half : (h + 1) * half] = product.reshape(half, tile, tile)
        leave(h).start()
        added = transposed_dot(jnp.concatenate(turned, axis=0), product)
        for k in range(n_fac):
            share = added[k * tile : (k + 1) * tile]
            sums[k] = sums[k] + share if h else share
    leave(0).wait()
    leave(1).wait()


def products(ids, marks, flags, ancestor, column, factors):
    n, cols, tile, _ = ancestor.shape
    n_fac = len(factors)
    out = jax.ShapeDtypeStruct((n // 2, tile, tile), BF16)
    memory = [pltpu.SMEM] * 3 + [pl.ANY] + [pltpu.VMEM] * (1 + n_fac)
    return pl.pallas_call(
        functools.partial(product_kernel, n_fac),
        out_shape=(out, out, jax.ShapeDtypeStruct((n_fac, tile, tile), F32)),
        in_specs=[pl.BlockSpec(memory_space=space) for space in memory],
        out_specs=[pl.BlockSpec(memory_space=space) for space in (pl.ANY, pl.ANY, pltpu.VMEM)],
        scratch_shapes=[
            pltpu.VMEM((n, cols, tile, tile), BF16),
            pltpu.VMEM((n, tile, tile), BF16),
            pltpu.SemaphoreType.DMA((n,)),
            pltpu.SemaphoreType.DMA((2,)),
        ],
        compiler_params=pltpu.CompilerParams(vmem_limit_bytes=60 << 20),
        cost_estimate=pl.CostEstimate(
            flops=2 * n * (cols + n_fac) * tile**3,
            bytes_accessed=2 * n * (cols + n_fac + 1) * tile**2,
            transcendentals=0,
        ),
    )(ids, marks, flags, ancestor, column, *factors)


def after(array, *earlier):
    return lax.optimization_barrier((array, *earlier))[0]


def shards(
    ancestor,
    tile_mask,
    member_one,
    member_two,
    factor_one,
    factor_two,
    link_block,
    inverse_one,
    inverse_two,
):
    nrow, ncol = lax.axis_size("row"), lax.axis_size("col")
    row, col = lax.axis_index("row"), lax.axis_index("col")
    rows, cols, tile = ancestor.shape[0], ancestor.shape[1], ancestor.shape[-1]
    group = ncol // nrow
    bits, row_bits = ncol.bit_length() - 1, nrow.bit_length() - 1
    owner = col // group
    at = lambda r, c: r * ncol + c
    everyone = [(r, c) for r in range(nrow) for c in range(ncol)]

    def over_chips(piece, *earlier):
        have = piece
        for k in range(2, nrow, 2):
            perm = [(at(c // group, c), at((c // group + k) % nrow, c)) for c in range(ncol)]
            got = after(lax.ppermute(piece, BOTH, perm), *earlier)
            have = jnp.where((row - owner) % nrow == k, got, have)
        return have

    def over_cores(have):
        perm = [
            (at(2 * y + c // group % 2, c), at(2 * y + 1 - c // group % 2, c))
            for y in range(nrow // 2)
            for c in range(ncol)
        ]
        return jnp.where((row - owner) % 2 == 0, have, lax.ppermute(have, BOTH, perm))

    def swap(array, bit):
        return lax.ppermute(array, BOTH, [(at(r, c), at(r, c ^ (1 << bit))) for r, c in everyone])

    def swap_rows(array, bit):
        return lax.ppermute(array, BOTH, [(at(r, c), at(r ^ (1 << bit), c)) for r, c in everyone])

    def pick(array, bit, other):
        split = array.reshape(array.shape[0] // 2, 2, *array.shape[1:])
        return lax.dynamic_slice_in_dim(split, (col >> bit & 1) ^ other, 1, 1)[:, 0].astype(F32)

    def merged(keep, got, bit, other):
        return pick(keep, bit, other) + pick(got, bit, other)

    flags_one = lax.dynamic_slice_in_dim(member_one, row * rows, rows, 0)
    flags_two = lax.dynamic_slice_in_dim(member_two, row * rows, rows, 0)
    marks = [
        (tile_mask * lax.dynamic_slice_in_dim(m, col * cols, cols, 0)[None]).reshape(-1)
        for m in (member_one, member_two)
    ]
    flags = [jnp.stack([flags_one, flags_one * flags_two], 1).reshape(-1), flags_two]
    ids = jnp.arange(rows // 2, dtype=jnp.int32) * 2
    ids = jnp.concatenate([ids + (1 - col % 2), ids + col % 2])

    piece_one, piece_two = pieces((col % group * cols)[None], factor_one, factor_two, cols)
    have_one = over_chips(piece_one, *marks, *flags, ids)
    have_two = over_chips(piece_two)
    column = over_cores(have_one)
    away, keep_one, sums_one = products(
        ids, marks[0], flags[0], ancestor, column, (factor_one, factor_two)
    )
    one = [swap(away, 0)]
    column = over_cores(after(have_two, keep_one))
    away, keep_two, sums_two = products(ids, marks[1], flags[1], ancestor, column, (factor_two,))
    two = [swap(away, 0)]

    for bit in range(1, bits):
        away = merged(keep_one, one[-1], bit, 1).astype(BF16)
        keep_one = merged(keep_one, one[-1], bit, 0)
        one.append(swap(away, bit))
        away = merged(keep_two, two[-1], bit, 1).astype(BF16)
        keep_two = merged(keep_two, two[-1], bit, 0)
        two.append(swap(away, bit))

    sums = jnp.concatenate([sums_one, sums_two])
    shape = sums.shape
    part = sums.reshape(-1, tile)
    for bit in range(row_bits):
        half = part.shape[0] // 2
        mine = row >> bit & 1
        if bit == row_bits - 1:
            part = after(part, one[0])
        got = swap_rows(lax.dynamic_slice_in_dim(part, (1 - mine) * half, half, 0).astype(BF16), bit)
        part = lax.dynamic_slice_in_dim(part, mine * half, half, 0) + got.astype(F32)
    part = part.astype(BF16)
    steps = [one[0], two[0]] + one[1:-1]
    for bit in range(bits):
        got = swap(after(part, steps[bit]), bit)
        part = (part.astype(F32) + got.astype(F32)).astype(BF16)
    for bit in reversed(range(row_bits)):
        got = swap_rows(after(part, two[-1], one[-1]) if bit == 0 else after(part, two[-2]), bit)
        low = (row >> bit & 1) == 0
        part = jnp.concatenate([jnp.where(low, part, got), jnp.where(low, got, part)])

    column_one, column_two = small_kernel(
        column_kernel,
        2,
        1,
        tile,
        (
            member_one,
            member_two,
            (row * rows + col)[None],
            link_block,
            *(a[0] for a in (keep_one, one[-1], keep_two, two[-1])),
        ),
        3,
    )
    diag_one, cross_block, diag_two = small_kernel(
        diagonal_kernel, 3, 3, tile, (part.reshape(shape), link_block, inverse_one, inverse_two)
    )
    return (column_one[None], column_two[None], diag_one, cross_block, diag_two)


def solution(mesh):
    in_specs = (
        P("row", "col", None, None),
        P("row", "col"),
        P(),
        P(),
        P("row", None, None),
        P("row", None, None),
        P(),
        P(),
        P(),
    )
    out_specs = (P(("row", "col"), None, None), P(("row", "col"), None, None), P(), P(), P())
    return jax.shard_map(shards, mesh=mesh, in_specs=in_specs, out_specs=out_specs, check_vma=False)
```

```python
import jax
import jax.numpy as jnp
from jax import lax
from jax.experimental import pallas as pl
from jax.experimental.pallas import tpu as pltpu
from jax.sharding import PartitionSpec as P

F32, BF16 = jnp.float32, jnp.bfloat16
BOTH = ("row", "col")


def transposed_dot(a, b):
    return lax.dot_general(a, b, (((0,), (0,)), ((), ())), preferred_element_type=F32)


def column_kernel(first, second, place, link, keep_one, got_one, keep_two, got_two, column_one, column_two):
    member_one, member_two = (m[place[0]].astype(F32) for m in (first, second))
    one = keep_one[...].astype(F32) + got_one[...].astype(F32)
    column_one[...] = (-member_one * one).astype(BF16)
    two = keep_two[...].astype(F32) + got_two[...].astype(F32)
    two += jnp.dot(column_one[...], link[...], preferred_element_type=F32)
    column_two[...] = (-member_two * two).astype(BF16)


def diagonal_kernel(sums, link, inverse_one, inverse_two, diag_one, cross, diag_two):
    diag_one[...] = (inverse_one[...] + sums[0].astype(F32)).astype(BF16)
    step = jnp.dot(diag_one[...], link[...], preferred_element_type=F32)
    cross[...] = (sums[1].astype(F32) - step).astype(BF16)
    two = inverse_two[...] + sums[2].astype(F32) - transposed_dot(sums[1], link[...])
    diag_two[...] = (two - transposed_dot(link[...], cross[...])).astype(BF16)


def small_kernel(body, n_out, n_dots, tile, operands, scalars=0):
    memory = [pltpu.SMEM] * scalars + [pltpu.VMEM] * (len(operands) - scalars)
    return pl.pallas_call(
        body,
        out_shape=(jax.ShapeDtypeStruct((tile, tile), BF16),) * n_out,
        in_specs=[pl.BlockSpec(memory_space=space) for space in memory],
        out_specs=[pl.BlockSpec(memory_space=pltpu.VMEM)] * n_out,
        cost_estimate=pl.CostEstimate(
            flops=2 * n_dots * tile**3,
            bytes_accessed=4 * len(operands) * tile**2,
            transcendentals=0,
        ),
    )(*operands)


def after(array, *earlier):
    return lax.optimization_barrier((array, *earlier))[0]


def shards(
    ancestor,
    tile_mask,
    member_one,
    member_two,
    factor_one,
    factor_two,
    link_block,
    inverse_one,
    inverse_two,
):
    nrow, ncol = lax.axis_size("row"), lax.axis_size("col")
    row, col = lax.axis_index("row"), lax.axis_index("col")
    rows, cols, tile = ancestor.shape[0], ancestor.shape[1], ancestor.shape[-1]
    group = ncol // nrow
    bits, row_bits = ncol.bit_length() - 1, nrow.bit_length() - 1
    owner = col // group
    at = lambda r, c: r * ncol + c
    everyone = [(r, c) for r in range(nrow) for c in range(ncol)]

    def over_chips(piece, *earlier):
        have = piece
        for k in range(2, nrow, 2):
            perm = [(at(c // group, c), at((c // group + k) % nrow, c)) for c in range(ncol)]
            got = after(lax.ppermute(piece, BOTH, perm), *earlier)
            have = jnp.where((row - owner) % nrow == k, got, have)
        return have

    def over_cores(have):
        perm = [
            (at(2 * y + c // group % 2, c), at(2 * y + 1 - c // group % 2, c))
            for y in range(nrow // 2)
            for c in range(ncol)
        ]
        return jnp.where((row - owner) % 2 == 0, have, lax.ppermute(have, BOTH, perm))

    def swap(array, bit):
        return lax.ppermute(array, BOTH, [(at(r, c), at(r, c ^ (1 << bit))) for r, c in everyone])

    def swap_rows(array, bit):
        return lax.ppermute(array, BOTH, [(at(r, c), at(r ^ (1 << bit), c)) for r, c in everyone])

    def pick(array, bit, other):
        split = array.reshape(array.shape[0] // 2, 2, *array.shape[1:])
        return lax.dynamic_slice_in_dim(split, (col >> bit & 1) ^ other, 1, 1)[:, 0].astype(F32)

    def merged(keep, got, bit, other):
        return pick(keep, bit, other) + pick(got, bit, other)

    def part_of(array, start, size):
        return lax.dynamic_slice_in_dim(array, start, size, 0)

    def masked(marks, array):
        return jnp.where(marks.reshape(marks.shape + (1, 1)) > 0, array, jnp.zeros((), BF16))

    def products(marks, column):
        kept = masked(marks, ancestor)
        return jnp.einsum("ijab,jbc->iac", kept, column, preferred_element_type=F32).astype(BF16)

    def contraction(a, b):
        return jnp.einsum("sab,sac->bc", a, b, preferred_element_type=F32)

    flags_one, flags_two = (part_of(m, row * rows, rows) for m in (member_one, member_two))
    marks = [tile_mask * part_of(m, col * cols, cols)[None] for m in (member_one, member_two)]
    first, second = masked(flags_one, factor_one), masked(flags_two, factor_two)
    second_in_one = masked(flags_one, second)

    piece_one, piece_two = (part_of(f, col % group * cols, cols) for f in (factor_one, factor_two))
    have_one, have_two = over_chips(piece_one, *marks), over_chips(piece_two)
    keep_one = products(marks[0], over_cores(have_one))
    one = [swap(pick(keep_one, 0, 1).astype(BF16), 0)]
    sums_one = contraction(first, keep_one), contraction(keep_one, second_in_one)
    keep_two = products(marks[1], over_cores(after(have_two, keep_one)))
    two = [swap(pick(keep_two, 0, 1).astype(BF16), 0)]
    sums_two = contraction(second, keep_two)
    keep_one, keep_two = pick(keep_one, 0, 0), pick(keep_two, 0, 0)

    for bit in range(1, bits):
        away = merged(keep_one, one[-1], bit, 1).astype(BF16)
        keep_one = merged(keep_one, one[-1], bit, 0)
        one.append(swap(away, bit))
        away = merged(keep_two, two[-1], bit, 1).astype(BF16)
        keep_two = merged(keep_two, two[-1], bit, 0)
        two.append(swap(away, bit))

    sums = jnp.stack([*sums_one, sums_two])
    shape = sums.shape
    part = sums.reshape(-1, tile)
    for bit in range(row_bits):
        half = part.shape[0] // 2
        mine = row >> bit & 1
        if bit == row_bits - 1:
            part = after(part, one[0])
        got = swap_rows(lax.dynamic_slice_in_dim(part, (1 - mine) * half, half, 0).astype(BF16), bit)
        part = lax.dynamic_slice_in_dim(part, mine * half, half, 0) + got.astype(F32)
    part = part.astype(BF16)
    for bit in (*range(1, bits), 0):
        if bit != 1:
            part = after(part, one[1] if bit == 0 else two[0])
        got = swap(part, bit)
        part = (part.astype(F32) + got.astype(F32)).astype(BF16)
    for bit in reversed(range(row_bits)):
        got = swap_rows(after(part, two[-1], one[-1]) if bit == 0 else after(part, two[-2]), bit)
        low = (row >> bit & 1) == 0
        part = jnp.concatenate([jnp.where(low, part, got), jnp.where(low, got, part)])

    column_one, column_two = small_kernel(
        column_kernel,
        2,
        1,
        tile,
        (
            member_one,
            member_two,
            (row * rows + col)[None],
            link_block,
            *(a[0] for a in (keep_one, one[-1], keep_two, two[-1])),
        ),
        3,
    )
    diag_one, cross_block, diag_two = small_kernel(
        diagonal_kernel, 3, 3, tile, (part.reshape(shape), link_block, inverse_one, inverse_two)
    )
    return (column_one[None], column_two[None], diag_one, cross_block, diag_two)


def solution(mesh):
    in_specs = (
        P("row", "col", None, None),
        P("row", "col"),
        P(),
        P(),
        P("row", None, None),
        P("row", None, None),
        P(),
        P(),
        P(),
    )
    out_specs = (P(("row", "col"), None, None), P(("row", "col"), None, None), P(), P(), P())
    return jax.shard_map(shards, mesh=mesh, in_specs=in_specs, out_specs=out_specs, check_vma=False)
```

```python
import jax
import jax.numpy as jnp
from jax import lax
from jax.experimental import pallas as pl
from jax.experimental.pallas import tpu as pltpu
from jax.sharding import PartitionSpec as P

F32, BF16 = jnp.float32, jnp.bfloat16
BOTH = ("row", "col")


def transposed_dot(a, b):
    return lax.dot_general(a, b, (((0,), (0,)), ((), ())), preferred_element_type=F32)


def diagonal_kernel(sums, link, inverse_one, inverse_two, diag_one, cross, diag_two):
    diag_one[...] = (inverse_one[...] + sums[0].astype(F32)).astype(BF16)
    step = jnp.dot(diag_one[...], link[...], preferred_element_type=F32)
    cross[...] = (sums[1].astype(F32) - step).astype(BF16)
    two = inverse_two[...] + sums[2].astype(F32) - transposed_dot(sums[1], link[...])
    diag_two[...] = (two - transposed_dot(link[...], cross[...])).astype(BF16)


def small_kernel(body, n_out, n_dots, tile, operands, scalars=0):
    memory = [pltpu.SMEM] * scalars + [pltpu.VMEM] * (len(operands) - scalars)
    return pl.pallas_call(
        body,
        out_shape=(jax.ShapeDtypeStruct((tile, tile), BF16),) * n_out,
        in_specs=[pl.BlockSpec(memory_space=space) for space in memory],
        out_specs=[pl.BlockSpec(memory_space=pltpu.VMEM)] * n_out,
        cost_estimate=pl.CostEstimate(
            flops=2 * n_dots * tile**3,
            bytes_accessed=4 * len(operands) * tile**2,
            transcendentals=0,
        ),
    )(*operands)


def after(array, *earlier):
    return lax.optimization_barrier((array, *earlier))[0]


def shards(
    ancestor,
    tile_mask,
    member_one,
    member_two,
    factor_one,
    factor_two,
    link_block,
    inverse_one,
    inverse_two,
):
    nrow, ncol = lax.axis_size("row"), lax.axis_size("col")
    row, col = lax.axis_index("row"), lax.axis_index("col")
    rows, cols, tile = ancestor.shape[0], ancestor.shape[1], ancestor.shape[-1]
    group = ncol // nrow
    bits, row_bits = ncol.bit_length() - 1, nrow.bit_length() - 1
    owner = col // group
    at = lambda r, c: r * ncol + c
    everyone = [(r, c) for r in range(nrow) for c in range(ncol)]

    def over_chips(piece, *earlier):
        have = piece
        for k in range(2, nrow, 2):
            perm = [(at(c // group, c), at((c // group + k) % nrow, c)) for c in range(ncol)]
            got = after(lax.ppermute(piece, BOTH, perm), *earlier)
            have = jnp.where((row - owner) % nrow == k, got, have)
        return have

    def over_cores(have):
        perm = [
            (at(2 * y + c // group % 2, c), at(2 * y + 1 - c // group % 2, c))
            for y in range(nrow // 2)
            for c in range(ncol)
        ]
        return jnp.where((row - owner) % 2 == 0, have, lax.ppermute(have, BOTH, perm))

    def swap(array, bit):
        return lax.ppermute(array, BOTH, [(at(r, c), at(r, c ^ (1 << bit))) for r, c in everyone])

    def swap_rows(array, bit):
        return lax.ppermute(array, BOTH, [(at(r, c), at(r ^ (1 << bit), c)) for r, c in everyone])

    def pick(array, bits_left, bit, other):
        lower = 1 << bits_left.index(bit)
        split = array.reshape(-1, 2, lower, tile, tile)
        return lax.dynamic_slice_in_dim(split, (col >> bit & 1) ^ other, 1, 1).reshape(-1, tile, tile).astype(F32)

    def first_swap(array, order):
        left = list(range(bits))
        away, keep = (pick(array, left, order[0], other) for other in (1, 0))
        left.remove(order[0])
        return left, keep, [swap(away.astype(BF16), order[0])]

    def next_swap(left, keep, arrived, order):
        bit = order[len(arrived)]
        away, keep = (
            pick(keep, left, bit, other) + pick(arrived[-1], left, bit, other) for other in (1, 0)
        )
        left.remove(bit)
        arrived.append(swap(away.astype(BF16), bit))
        return keep

    def part_of(array, start, size):
        return lax.dynamic_slice_in_dim(array, start, size, 0)

    def masked(marks, array):
        return jnp.where(marks.reshape(marks.shape + (1, 1)) > 0, array, jnp.zeros((), BF16))

    def products(marks, column):
        kept = masked(marks, ancestor)
        return jnp.einsum("ijab,jbc->iac", kept, column, preferred_element_type=F32).astype(BF16)

    def contraction(a, b):
        return jnp.einsum("sab,sac->bc", a, b, preferred_element_type=F32)

    flags_one, flags_two = (part_of(m, row * rows, rows) for m in (member_one, member_two))
    marks = [tile_mask * part_of(m, col * cols, cols)[None] for m in (member_one, member_two)]
    first, second = masked(flags_one, factor_one), masked(flags_two, factor_two)
    second_in_one = masked(flags_one, second)

    piece_one, piece_two = (part_of(f, col % group * cols, cols) for f in (factor_one, factor_two))
    piece_one, piece_two = after(piece_one), after(piece_two)
    order_one, order_two = list(range(bits)), [1, 0, *range(2, bits)]
    have_one, have_two = over_chips(piece_one, *marks), over_chips(piece_two)
    all_one = products(marks[0], over_cores(have_one))
    left_one, keep_one, one = first_swap(all_one, order_one)
    column = over_cores(after(have_two, all_one))
    all_two = products(marks[1], column)
    left_two, keep_two, two = first_swap(all_two, order_two)
    all_one = after(all_one, all_two)
    sums = contraction(first, all_one), contraction(all_one, second_in_one), contraction(second, all_two)
    for _ in range(1, bits):
        keep_one = next_swap(left_one, keep_one, one, order_one)
        keep_two = next_swap(left_two, keep_two, two, order_two)

    sums = jnp.stack(sums)
    shape = sums.shape
    part = sums.reshape(-1, tile)
    for bit in range(row_bits):
        half = part.shape[0] // 2
        mine = row >> bit & 1
        got = swap_rows(lax.dynamic_slice_in_dim(part, (1 - mine) * half, half, 0).astype(BF16), bit)
        part = lax.dynamic_slice_in_dim(part, mine * half, half, 0) + got.astype(F32)
    part = part.astype(BF16)
    gates = [one[0], two[0], *one[1:]]
    for bit in range(bits):
        got = swap(after(part, gates[bit]), bit)
        part = (part.astype(F32) + got.astype(F32)).astype(BF16)
    for bit in reversed(range(row_bits)):
        got = swap_rows(after(part, one[-1] if bit == 0 else two[-2]), bit)
        low = (row >> bit & 1) == 0
        part = jnp.concatenate([jnp.where(low, part, got), jnp.where(low, got, part)])

    member_one, member_two = (m[row * rows + col].astype(F32) for m in (member_one, member_two))
    column_one = (-member_one * (keep_one[0] + one[-1][0].astype(F32))).astype(BF16)
    linked = jnp.dot(column_one, link_block, preferred_element_type=F32) + keep_two[0]
    column_two = (-member_two * (linked + two[-1][0].astype(F32))).astype(BF16)
    diag_one, cross_block, diag_two = small_kernel(
        diagonal_kernel, 3, 3, tile, (part.reshape(shape), link_block, inverse_one, inverse_two)
    )
    return (column_one[None], column_two[None], diag_one, cross_block, diag_two)


def solution(mesh):
    in_specs = (
        P("row", "col", None, None),
        P("row", "col"),
        P(),
        P(),
        P("row", None, None),
        P("row", None, None),
        P(),
        P(),
        P(),
    )
    out_specs = (P(("row", "col"), None, None), P(("row", "col"), None, None), P(), P(), P())
    return jax.shard_map(shards, mesh=mesh, in_specs=in_specs, out_specs=out_specs, check_vma=False)
```

```python
import jax
import jax.numpy as jnp
from jax import lax
from jax.experimental import pallas as pl
from jax.experimental.pallas import tpu as pltpu
from jax.sharding import PartitionSpec as P

F32, BF16 = jnp.float32, jnp.bfloat16
BOTH = ("row", "col")


def transposed_dot(a, b):
    return lax.dot_general(a, b, (((0,), (0,)), ((), ())), preferred_element_type=F32)


def diagonal_kernel(sums, link, inverse_one, inverse_two, diag_one, cross, diag_two):
    diag_one[...] = (inverse_one[...] + sums[0].astype(F32)).astype(BF16)
    step = jnp.dot(diag_one[...], link[...], preferred_element_type=F32)
    cross[...] = (sums[1].astype(F32) - step).astype(BF16)
    two = inverse_two[...] + sums[2].astype(F32) - transposed_dot(sums[1], link[...])
    diag_two[...] = (two - transposed_dot(link[...], cross[...])).astype(BF16)


def small_kernel(body, n_out, n_dots, tile, operands, scalars=0):
    memory = [pltpu.SMEM] * scalars + [pltpu.VMEM] * (len(operands) - scalars)
    return pl.pallas_call(
        body,
        out_shape=(jax.ShapeDtypeStruct((tile, tile), BF16),) * n_out,
        in_specs=[pl.BlockSpec(memory_space=space) for space in memory],
        out_specs=[pl.BlockSpec(memory_space=pltpu.VMEM)] * n_out,
        cost_estimate=pl.CostEstimate(
            flops=2 * n_dots * tile**3,
            bytes_accessed=4 * len(operands) * tile**2,
            transcendentals=0,
        ),
    )(*operands)


def after(array, *earlier):
    return lax.optimization_barrier((array, *earlier))[0]


def shards(
    ancestor,
    tile_mask,
    member_one,
    member_two,
    factor_one,
    factor_two,
    link_block,
    inverse_one,
    inverse_two,
):
    nrow, ncol = lax.axis_size("row"), lax.axis_size("col")
    row, col = lax.axis_index("row"), lax.axis_index("col")
    rows, cols, tile = ancestor.shape[0], ancestor.shape[1], ancestor.shape[-1]
    group = ncol // nrow
    bits, row_bits = ncol.bit_length() - 1, nrow.bit_length() - 1
    owner = col // group
    at = lambda r, c: r * ncol + c
    everyone = [(r, c) for r in range(nrow) for c in range(ncol)]

    def over_chips(piece, *earlier):
        have = piece
        for k in range(2, nrow, 2):
            perm = [(at(c // group, c), at((c // group + k) % nrow, c)) for c in range(ncol)]
            got = after(lax.ppermute(piece, BOTH, perm), *earlier)
            have = jnp.where((row - owner) % nrow == k, got, have)
        return have

    def over_cores(have):
        perm = [
            (at(2 * y + c // group % 2, c), at(2 * y + 1 - c // group % 2, c))
            for y in range(nrow // 2)
            for c in range(ncol)
        ]
        return jnp.where((row - owner) % 2 == 0, have, lax.ppermute(have, BOTH, perm))

    def swap(array, bit):
        return lax.ppermute(array, BOTH, [(at(r, c), at(r, c ^ (1 << bit))) for r, c in everyone])

    def swap_rows(array, bit):
        return lax.ppermute(array, BOTH, [(at(r, c), at(r ^ (1 << bit), c)) for r, c in everyone])

    def pick(array, bits_left, bit, other):
        lower = 1 << bits_left.index(bit)
        split = array.reshape(-1, 2, lower, tile, tile)
        return lax.dynamic_slice_in_dim(split, (col >> bit & 1) ^ other, 1, 1).reshape(-1, tile, tile).astype(F32)

    def first_swap(array, order):
        left = list(range(bits))
        away, keep = (pick(array, left, order[0], other) for other in (1, 0))
        left.remove(order[0])
        return left, keep, [swap(away.astype(BF16), order[0])]

    def next_swap(left, keep, arrived, order):
        bit = order[len(arrived)]
        away, keep = (
            pick(keep, left, bit, other) + pick(arrived[-1], left, bit, other) for other in (1, 0)
        )
        left.remove(bit)
        arrived.append(swap(away.astype(BF16), bit))
        return keep

    def part_of(array, start, size):
        return lax.dynamic_slice_in_dim(array, start, size, 0)

    def masked(marks, array):
        return jnp.where(marks.reshape(marks.shape + (1, 1)) > 0, array, jnp.zeros((), BF16))

    def products(marks, column):
        kept = masked(marks, ancestor)
        return jnp.einsum("ijab,jbc->iac", kept, column, preferred_element_type=F32).astype(BF16)

    def contraction(a, b):
        return jnp.einsum("sab,sac->bc", a, b, preferred_element_type=F32)

    flags_one, flags_two = (part_of(m, row * rows, rows) for m in (member_one, member_two))
    marks = [tile_mask * part_of(m, col * cols, cols)[None] for m in (member_one, member_two)]
    first, second = masked(flags_one, factor_one), masked(flags_two, factor_two)
    second_in_one = masked(flags_one, second)

    piece_one, piece_two = (part_of(f, col % group * cols, cols) for f in (factor_one, factor_two))
    piece_one, piece_two = after(piece_one), after(piece_two)
    order_one, order_two = list(range(bits)), [1, 0, *range(2, bits)]
    have_one, have_two = over_chips(piece_one, *marks, flags_one, flags_two), over_chips(piece_two)
    all_one = products(marks[0], over_cores(have_one))
    left_one, keep_one, one = first_swap(all_one, order_one)
    all_two = products(marks[1], over_cores(after(have_two, all_one)))
    left_two, keep_two, two = first_swap(all_two, order_two)
    sums = contraction(first, all_one), contraction(all_one, second_in_one), contraction(second, all_two)
    for _ in range(1, bits):
        keep_one = next_swap(left_one, keep_one, one, order_one)
        keep_two = next_swap(left_two, keep_two, two, order_two)

    sums = jnp.stack(sums)
    shape = sums.shape
    part = sums.reshape(-1, tile)
    for bit in range(row_bits):
        half = part.shape[0] // 2
        mine = row >> bit & 1
        got = swap_rows(lax.dynamic_slice_in_dim(part, (1 - mine) * half, half, 0).astype(BF16), bit)
        part = lax.dynamic_slice_in_dim(part, mine * half, half, 0) + got.astype(F32)
    part = part.astype(BF16)
    gates = [one[0], two[0], *one[1:]]
    for bit, gate in zip((*range(2, bits), 0, 1), gates):
        got = swap(after(part, gate), bit)
        part = (part.astype(F32) + got.astype(F32)).astype(BF16)
    for bit in reversed(range(row_bits)):
        got = swap_rows(after(part, one[-1] if bit == 0 else two[-2]), bit)
        low = (row >> bit & 1) == 0
        part = jnp.concatenate([jnp.where(low, part, got), jnp.where(low, got, part)])

    member_one, member_two = (m[row * rows + col].astype(F32) for m in (member_one, member_two))
    column_one = (-member_one * (keep_one[0] + one[-1][0].astype(F32))).astype(BF16)
    linked = jnp.dot(column_one, link_block, preferred_element_type=F32) + keep_two[0]
    column_two = (-member_two * (linked + two[-1][0].astype(F32))).astype(BF16)
    diag_one, cross_block, diag_two = small_kernel(
        diagonal_kernel, 3, 3, tile, (part.reshape(shape), link_block, inverse_one, inverse_two)
    )
    return (column_one[None], column_two[None], diag_one, cross_block, diag_two)


def solution(mesh):
    in_specs = (
        P("row", "col", None, None),
        P("row", "col"),
        P(),
        P(),
        P("row", None, None),
        P("row", None, None),
        P(),
        P(),
        P(),
    )
    out_specs = (P(("row", "col"), None, None), P(("row", "col"), None, None), P(), P(), P())
    return jax.shard_map(shards, mesh=mesh, in_specs=in_specs, out_specs=out_specs, check_vma=False)
```

```python
import jax
import jax.numpy as jnp
from jax import lax
from jax.experimental import pallas as pl
from jax.experimental.pallas import tpu as pltpu
from jax.sharding import PartitionSpec as P

F32, BF16 = jnp.float32, jnp.bfloat16
BOTH = ("row", "col")


def transposed_dot(a, b):
    return lax.dot_general(a, b, (((0,), (0,)), ((), ())), preferred_element_type=F32)


def diagonal_kernel(place, mine, other, link, inverse_one, inverse_two, diag_one, cross, diag_two):
    low = place[0] == 0
    low, high = jnp.where(low, mine[...], other[...]), jnp.where(low, other[...], mine[...])
    sums = jnp.concatenate([low, high]).reshape(3, *link.shape)
    diag_one[...] = (inverse_one[...] + sums[0].astype(F32)).astype(BF16)
    step = jnp.dot(diag_one[...], link[...], preferred_element_type=F32)
    cross[...] = (sums[1].astype(F32) - step).astype(BF16)
    two = inverse_two[...] + sums[2].astype(F32) - transposed_dot(sums[1], link[...])
    diag_two[...] = (two - transposed_dot(link[...], cross[...])).astype(BF16)


def small_kernel(body, n_out, n_dots, tile, operands, scalars=0):
    memory = [pltpu.SMEM] * scalars + [pltpu.VMEM] * (len(operands) - scalars)
    return pl.pallas_call(
        body,
        out_shape=(jax.ShapeDtypeStruct((tile, tile), BF16),) * n_out,
        in_specs=[pl.BlockSpec(memory_space=space) for space in memory],
        out_specs=[pl.BlockSpec(memory_space=pltpu.VMEM)] * n_out,
        cost_estimate=pl.CostEstimate(
            flops=2 * n_dots * tile**3,
            bytes_accessed=4 * len(operands) * tile**2,
            transcendentals=0,
        ),
    )(*operands)


def after(array, *earlier):
    return lax.optimization_barrier((array, *earlier))[0]


def shards(
    ancestor,
    tile_mask,
    member_one,
    member_two,
    factor_one,
    factor_two,
    link_block,
    inverse_one,
    inverse_two,
):
    nrow, ncol = lax.axis_size("row"), lax.axis_size("col")
    row, col = lax.axis_index("row"), lax.axis_index("col")
    rows, cols, tile = ancestor.shape[0], ancestor.shape[1], ancestor.shape[-1]
    group = ncol // nrow
    bits, row_bits = ncol.bit_length() - 1, nrow.bit_length() - 1
    owner = col // group
    at = lambda r, c: r * ncol + c
    everyone = [(r, c) for r in range(nrow) for c in range(ncol)]

    def over_chips(piece, *earlier):
        have = piece
        for k in range(2, nrow, 2):
            perm = [(at(c // group, c), at((c // group + k) % nrow, c)) for c in range(ncol)]
            got = after(lax.ppermute(piece, BOTH, perm), *earlier)
            have = jnp.where((row - owner) % nrow == k, got, have)
        return have

    def over_cores(have):
        perm = [
            (at(2 * y + c // group % 2, c), at(2 * y + 1 - c // group % 2, c))
            for y in range(nrow // 2)
            for c in range(ncol)
        ]
        return jnp.where((row - owner) % 2 == 0, have, lax.ppermute(have, BOTH, perm))

    def swap(array, bit):
        return lax.ppermute(array, BOTH, [(at(r, c), at(r, c ^ (1 << bit))) for r, c in everyone])

    def swap_rows(array, bit):
        return lax.ppermute(array, BOTH, [(at(r, c), at(r ^ (1 << bit), c)) for r, c in everyone])

    def pick(array, bit, other):
        split = array.reshape(-1, 2, tile, tile)
        return lax.dynamic_slice_in_dim(split, (col >> bit & 1) ^ other, 1, 1)[:, 0].astype(F32)

    def first_swap(array, *earlier):
        away, keep = (pick(array, 0, other) for other in (1, 0))
        return keep, [swap(after(away.astype(BF16), *earlier), 0)]

    def next_swap(keep, arrived):
        bit = len(arrived)
        away, keep = (pick(keep, bit, other) + pick(arrived[-1], bit, other) for other in (1, 0))
        arrived.append(swap(away.astype(BF16), bit))
        return keep

    def part_of(array, start, size):
        return lax.dynamic_slice_in_dim(array, start, size, 0)

    def masked(marks, array):
        return jnp.where(marks.reshape(marks.shape + (1, 1)) > 0, array, jnp.zeros((), BF16))

    def products(marks, column):
        kept = masked(marks, ancestor)
        return jnp.einsum("ijab,jbc->iac", kept, column, preferred_element_type=F32).astype(BF16)

    def contraction(a, b):
        return jnp.einsum("sab,sac->bc", a, b, preferred_element_type=F32)

    flags_one, flags_two = (part_of(m, row * rows, rows) for m in (member_one, member_two))
    marks = [tile_mask * part_of(m, col * cols, cols)[None] for m in (member_one, member_two)]
    first, second = masked(flags_one, factor_one), masked(flags_two, factor_two)
    second_in_one = masked(flags_one, second)

    piece_one, piece_two = (part_of(f, col % group * cols, cols) for f in (factor_one, factor_two))
    piece_one, piece_two = after(piece_one), after(piece_two)
    have_one, have_two = over_chips(piece_one, *marks, flags_one, flags_two), over_chips(piece_two)
    all_one = products(marks[0], over_cores(have_one))
    keep_one, one = first_swap(all_one)
    all_two = products(marks[1], over_cores(after(have_two, all_one)))
    keep_two, two = first_swap(all_two, one[0])
    sums = contraction(first, all_one), contraction(all_one, second_in_one), contraction(second, all_two)
    for _ in range(1, bits):
        keep_one = next_swap(keep_one, one)
        keep_two = next_swap(keep_two, two)

    sums = jnp.stack(sums)
    part = sums.reshape(-1, tile)
    for bit in range(row_bits):
        half = part.shape[0] // 2
        mine = row >> bit & 1
        got = swap_rows(lax.dynamic_slice_in_dim(part, (1 - mine) * half, half, 0).astype(BF16), bit)
        part = lax.dynamic_slice_in_dim(part, mine * half, half, 0) + got.astype(F32)
    part = part.astype(BF16)
    gates = [one[0], *one[1:-1], two[0]]
    for bit, gate in zip(reversed(range(bits)), gates):
        got = swap(after(part, gate), bit)
        part = (part.astype(F32) + got.astype(F32)).astype(BF16)
    for bit in reversed(range(row_bits)):
        got = swap_rows(after(part, *((one[-1], two[-2]) if bit == 0 else ())), bit)
        if bit:
            low = (row >> bit & 1) == 0
            part = jnp.concatenate([jnp.where(low, part, got), jnp.where(low, got, part)])

    member_one, member_two = (m[row * rows + col].astype(F32) for m in (member_one, member_two))
    column_one = (-member_one * (keep_one[0] + one[-1][0].astype(F32))).astype(BF16)
    linked = jnp.dot(column_one, link_block, preferred_element_type=F32) + keep_two[0]
    column_two = (-member_two * (linked + two[-1][0].astype(F32))).astype(BF16)
    diag_one, cross_block, diag_two = small_kernel(
        diagonal_kernel,
        3,
        3,
        tile,
        ((row & 1)[None], part, got, link_block, inverse_one, inverse_two),
        1,
    )
    return (column_one[None], column_two[None], diag_one, cross_block, diag_two)


def solution(mesh):
    in_specs = (
        P("row", "col", None, None),
        P("row", "col"),
        P(),
        P(),
        P("row", None, None),
        P("row", None, None),
        P(),
        P(),
        P(),
    )
    out_specs = (P(("row", "col"), None, None), P(("row", "col"), None, None), P(), P(), P())
    return jax.shard_map(shards, mesh=mesh, in_specs=in_specs, out_specs=out_specs, check_vma=False)
```

```python
import jax
import jax.numpy as jnp
from jax import lax
from jax.experimental import pallas as pl
from jax.experimental.pallas import tpu as pltpu
from jax.sharding import PartitionSpec as P

F32, BF16 = jnp.float32, jnp.bfloat16
BOTH = ("row", "col")


def transposed_dot(a, b):
    return lax.dot_general(a, b, (((0,), (0,)), ((), ())), preferred_element_type=F32)


def diagonal_kernel(place, mine, other, link, inverse_one, inverse_two, diag_one, cross, diag_two):
    low = place[0] == 0
    low, high = jnp.where(low, mine[...], other[...]), jnp.where(low, other[...], mine[...])
    sums = jnp.concatenate([low, high]).reshape(3, *link.shape)
    diag_one[...] = (inverse_one[...] + sums[0].astype(F32)).astype(BF16)
    step = jnp.dot(diag_one[...], link[...], preferred_element_type=F32)
    cross[...] = (sums[1].astype(F32) - step).astype(BF16)
    two = inverse_two[...] + sums[2].astype(F32) - transposed_dot(sums[1], link[...])
    diag_two[...] = (two - transposed_dot(link[...], cross[...])).astype(BF16)


def small_kernel(body, n_out, n_dots, tile, operands, scalars=0):
    memory = [pltpu.SMEM] * scalars + [pltpu.VMEM] * (len(operands) - scalars)
    return pl.pallas_call(
        body,
        out_shape=(jax.ShapeDtypeStruct((tile, tile), BF16),) * n_out,
        in_specs=[pl.BlockSpec(memory_space=space) for space in memory],
        out_specs=[pl.BlockSpec(memory_space=pltpu.VMEM)] * n_out,
        cost_estimate=pl.CostEstimate(
            flops=2 * n_dots * tile**3,
            bytes_accessed=4 * len(operands) * tile**2,
            transcendentals=0,
        ),
    )(*operands)


def after(array, *earlier):
    return lax.optimization_barrier((array, *earlier))[0]


def shards(
    ancestor,
    tile_mask,
    member_one,
    member_two,
    factor_one,
    factor_two,
    link_block,
    inverse_one,
    inverse_two,
):
    nrow, ncol = lax.axis_size("row"), lax.axis_size("col")
    row, col = lax.axis_index("row"), lax.axis_index("col")
    rows, cols, tile = ancestor.shape[0], ancestor.shape[1], ancestor.shape[-1]
    group = ncol // nrow
    bits, row_bits = ncol.bit_length() - 1, nrow.bit_length() - 1
    owner = col // group
    at = lambda r, c: r * ncol + c
    everyone = [(r, c) for r in range(nrow) for c in range(ncol)]

    def over_chips(piece, *earlier):
        have = piece
        for k in range(2, nrow, 2):
            perm = [(at(c // group, c), at((c // group + k) % nrow, c)) for c in range(ncol)]
            got = after(lax.ppermute(piece, BOTH, perm), *earlier)
            have = jnp.where((row - owner) % nrow == k, got, have)
        return have

    def over_cores(have):
        perm = [
            (at(2 * y + c // group % 2, c), at(2 * y + 1 - c // group % 2, c))
            for y in range(nrow // 2)
            for c in range(ncol)
        ]
        return jnp.where((row - owner) % 2 == 0, have, lax.ppermute(have, BOTH, perm))

    def swap(array, bit):
        return lax.ppermute(array, BOTH, [(at(r, c), at(r, c ^ (1 << bit))) for r, c in everyone])

    def swap_rows(array, bit):
        return lax.ppermute(array, BOTH, [(at(r, c), at(r ^ (1 << bit), c)) for r, c in everyone])

    def pick(array, bit, other):
        split = array.reshape(-1, 2, tile, tile)
        return lax.dynamic_slice_in_dim(split, (col >> bit & 1) ^ other, 1, 1)[:, 0].astype(F32)

    def first_swap(array, *earlier):
        away, keep = (pick(array, 0, other) for other in (1, 0))
        return keep, [swap(after(away.astype(BF16), *earlier), 0)]

    def next_swap(keep, arrived):
        bit = len(arrived)
        away, keep = (pick(keep, bit, other) + pick(arrived[-1], bit, other) for other in (1, 0))
        arrived.append(swap(away.astype(BF16), bit))
        return keep

    def part_of(array, start, size):
        return lax.dynamic_slice_in_dim(array, start, size, 0)

    def masked(marks, array):
        return jnp.where(marks.reshape(marks.shape + (1, 1)) > 0, array, jnp.zeros((), BF16))

    def products(marks, column):
        kept = masked(marks, ancestor)
        return jnp.einsum("ijab,jbc->iac", kept, column, preferred_element_type=F32).astype(BF16)

    def contraction(a, b):
        return jnp.einsum("sab,sac->bc", a, b, preferred_element_type=F32)

    flags_one, flags_two = (part_of(m, row * rows, rows) for m in (member_one, member_two))
    marks = [tile_mask * part_of(m, col * cols, cols)[None] for m in (member_one, member_two)]
    first, second = masked(flags_one, factor_one), masked(flags_two, factor_two)
    second_in_one = masked(flags_one, second)

    piece_one, piece_two = (part_of(f, col % group * cols, cols) for f in (factor_one, factor_two))
    piece_one, piece_two = after(piece_one), after(piece_two)
    have_one, have_two = over_chips(piece_one, *marks, flags_one, flags_two), over_chips(piece_two)
    all_one = products(marks[0], over_cores(have_one))
    keep_one, one = first_swap(all_one)
    all_two = products(marks[1], over_cores(after(have_two, all_one)))
    keep_two, two = first_swap(all_two, one[0])
    sums = contraction(first, all_one), contraction(all_one, second_in_one), contraction(second, all_two)
    for _ in range(1, bits):
        keep_one = next_swap(keep_one, one)
        keep_two = next_swap(keep_two, two)

    sums = jnp.stack(sums)
    part = sums.reshape(-1, tile)
    for bit in range(row_bits):
        half = part.shape[0] // 2
        mine = row >> bit & 1
        got = swap_rows(lax.dynamic_slice_in_dim(part, (1 - mine) * half, half, 0).astype(BF16), bit)
        part = lax.dynamic_slice_in_dim(part, mine * half, half, 0) + got.astype(F32)
    part = part.astype(BF16)
    gates = [one[0], two[0], *one[1:]]
    for bit, gate in zip(reversed(range(bits)), gates):
        got = swap(after(part, gate), bit)
        part = (part.astype(F32) + got.astype(F32)).astype(BF16)
    for bit in reversed(range(row_bits)):
        got = swap_rows(after(part, one[-1] if bit == 0 else two[-2]), bit)
        if bit:
            low = (row >> bit & 1) == 0
            part = jnp.concatenate([jnp.where(low, part, got), jnp.where(low, got, part)])

    diag_one, cross_block, diag_two = small_kernel(
        diagonal_kernel,
        3,
        3,
        tile,
        ((row & 1)[None], part, got, link_block, inverse_one, inverse_two),
        1,
    )
    member_one, member_two = (m[row * rows + col].astype(F32) for m in (member_one, member_two))
    column_one = (-member_one * (keep_one[0] + one[-1][0].astype(F32))).astype(BF16)
    linked = jnp.dot(column_one, link_block, preferred_element_type=F32) + keep_two[0]
    column_two = (-member_two * (linked + after(two[-1], diag_two)[0].astype(F32))).astype(BF16)
    return (column_one[None], column_two[None], diag_one, cross_block, diag_two)


def solution(mesh):
    in_specs = (
        P("row", "col", None, None),
        P("row", "col"),
        P(),
        P(),
        P("row", None, None),
        P("row", None, None),
        P(),
        P(),
        P(),
    )
    out_specs = (P(("row", "col"), None, None), P(("row", "col"), None, None), P(), P(), P())
    return jax.shard_map(shards, mesh=mesh, in_specs=in_specs, out_specs=out_specs, check_vma=False)
```

```python
import jax
import jax.numpy as jnp
from jax import lax
from jax.experimental import pallas as pl
from jax.experimental.pallas import tpu as pltpu
from jax.sharding import PartitionSpec as P

F32, BF16 = jnp.float32, jnp.bfloat16
BOTH = ("row", "col")


def transposed_dot(a, b):
    return lax.dot_general(a, b, (((0,), (0,)), ((), ())), preferred_element_type=F32)


def diagonal_kernel(place, mine, other, link, inverse_one, inverse_two, diag_one, cross, diag_two):
    low = place[0] == 0
    low, high = jnp.where(low, mine[...], other[...]), jnp.where(low, other[...], mine[...])
    sums = jnp.concatenate([low, high]).reshape(3, *link.shape)
    diag_one[...] = (inverse_one[...] + sums[0].astype(F32)).astype(BF16)
    step = jnp.dot(diag_one[...], link[...], preferred_element_type=F32)
    cross[...] = (sums[1].astype(F32) - step).astype(BF16)
    two = inverse_two[...] + sums[2].astype(F32) - transposed_dot(sums[1], link[...])
    diag_two[...] = (two - transposed_dot(link[...], cross[...])).astype(BF16)


def small_kernel(body, n_out, n_dots, tile, operands, scalars=0):
    memory = [pltpu.SMEM] * scalars + [pltpu.VMEM] * (len(operands) - scalars)
    return pl.pallas_call(
        body,
        out_shape=(jax.ShapeDtypeStruct((tile, tile), BF16),) * n_out,
        in_specs=[pl.BlockSpec(memory_space=space) for space in memory],
        out_specs=[pl.BlockSpec(memory_space=pltpu.VMEM)] * n_out,
        cost_estimate=pl.CostEstimate(
            flops=2 * n_dots * tile**3,
            bytes_accessed=4 * len(operands) * tile**2,
            transcendentals=0,
        ),
    )(*operands)


def after(array, *earlier):
    return lax.optimization_barrier((array, *earlier))[0]


def shards(
    ancestor,
    tile_mask,
    member_one,
    member_two,
    factor_one,
    factor_two,
    link_block,
    inverse_one,
    inverse_two,
):
    nrow, ncol = lax.axis_size("row"), lax.axis_size("col")
    row, col = lax.axis_index("row"), lax.axis_index("col")
    rows, cols, tile = ancestor.shape[0], ancestor.shape[1], ancestor.shape[-1]
    group = ncol // nrow
    bits, row_bits = ncol.bit_length() - 1, nrow.bit_length() - 1
    owner = col // group
    at = lambda r, c: r * ncol + c
    everyone = [(r, c) for r in range(nrow) for c in range(ncol)]

    def over_chips(piece, *earlier):
        have = piece
        for k in range(2, nrow, 2):
            perm = [(at(c // group, c), at((c // group + k) % nrow, c)) for c in range(ncol)]
            got = after(lax.ppermute(piece, BOTH, perm), *earlier)
            have = jnp.where((row - owner) % nrow == k, got, have)
        return have

    def over_cores(have):
        perm = [
            (at(2 * y + c // group % 2, c), at(2 * y + 1 - c // group % 2, c))
            for y in range(nrow // 2)
            for c in range(ncol)
        ]
        return jnp.where((row - owner) % 2 == 0, have, lax.ppermute(have, BOTH, perm))

    def swap(array, bit):
        return lax.ppermute(array, BOTH, [(at(r, c), at(r, c ^ (1 << bit))) for r, c in everyone])

    def swap_rows(array, bit):
        return lax.ppermute(array, BOTH, [(at(r, c), at(r ^ (1 << bit), c)) for r, c in everyone])

    def pick(array, bit, other):
        split = array.reshape(-1, 2, tile, tile)
        return lax.dynamic_slice_in_dim(split, (col >> bit & 1) ^ other, 1, 1)[:, 0].astype(F32)

    def first_swap(array, *earlier):
        away, keep = (pick(array, 0, other) for other in (1, 0))
        return keep, [swap(after(away.astype(BF16), *earlier), 0)]

    def next_swap(keep, arrived):
        bit = len(arrived)
        away, keep = (pick(keep, bit, other) + pick(arrived[-1], bit, other) for other in (1, 0))
        arrived.append(swap(away.astype(BF16), bit))
        return keep

    def part_of(array, start, size):
        return lax.dynamic_slice_in_dim(array, start, size, 0)

    def masked(marks, array):
        return jnp.where(marks.reshape(marks.shape + (1, 1)) > 0, array, jnp.zeros((), BF16))

    def products(marks, column):
        kept = masked(marks, ancestor)
        return jnp.einsum("ijab,jbc->iac", kept, column, preferred_element_type=F32).astype(BF16)

    def contraction(a, b):
        return jnp.einsum("sab,sac->bc", a, b, preferred_element_type=F32)

    flags_one, flags_two = (part_of(m, row * rows, rows) for m in (member_one, member_two))
    marks = [tile_mask * part_of(m, col * cols, cols)[None] for m in (member_one, member_two)]
    first, second = masked(flags_one, factor_one), masked(flags_two, factor_two)
    second_in_one = masked(flags_one, second)

    piece_one, piece_two = (part_of(f, col % group * cols, cols) for f in (factor_one, factor_two))
    piece_one, piece_two = after(piece_one), after(piece_two)
    have_one, have_two = over_chips(piece_one, *marks, flags_one, flags_two), over_chips(piece_two)
    all_one = products(marks[0], over_cores(have_one))
    keep_one, one = first_swap(all_one)
    all_two = products(marks[1], over_cores(after(have_two, all_one)))
    keep_two, two = first_swap(all_two)
    sums = contraction(first, all_one), contraction(all_one, second_in_one), contraction(second, all_two)
    for _ in range(1, bits):
        keep_one = next_swap(keep_one, one)
        keep_two = next_swap(keep_two, two)

    sums = jnp.stack(sums)
    part = sums.reshape(-1, tile)
    for bit in range(row_bits):
        half = part.shape[0] // 2
        mine = row >> bit & 1
        got = swap_rows(lax.dynamic_slice_in_dim(part, (1 - mine) * half, half, 0).astype(BF16), bit)
        part = lax.dynamic_slice_in_dim(part, mine * half, half, 0) + got.astype(F32)
    part = part.astype(BF16)
    gates = {bits - 1: one[:1], 0: [two[0], *one[1:-1]]}
    for bit in reversed(range(bits)):
        got = swap(after(part, *gates.get(bit, ())), bit)
        part = (part.astype(F32) + got.astype(F32)).astype(BF16)
    for bit in reversed(range(row_bits)):
        got = swap_rows(after(part, one[-1] if bit == 0 else two[-2]), bit)
        if bit:
            low = (row >> bit & 1) == 0
            part = jnp.concatenate([jnp.where(low, part, got), jnp.where(low, got, part)])

    diag_one, cross_block, diag_two = small_kernel(
        diagonal_kernel,
        3,
        3,
        tile,
        ((row & 1)[None], part, got, link_block, inverse_one, inverse_two),
        1,
    )
    member_one, member_two = (m[row * rows + col].astype(F32) for m in (member_one, member_two))
    column_one = (-member_one * (keep_one[0] + one[-1][0].astype(F32))).astype(BF16)
    linked = jnp.dot(column_one, link_block, preferred_element_type=F32) + keep_two[0]
    column_two = (-member_two * (linked + after(two[-1], diag_two)[0].astype(F32))).astype(BF16)
    return (column_one[None], column_two[None], diag_one, cross_block, diag_two)


def solution(mesh):
    in_specs = (
        P("row", "col", None, None),
        P("row", "col"),
        P(),
        P(),
        P("row", None, None),
        P("row", None, None),
        P(),
        P(),
        P(),
    )
    out_specs = (P(("row", "col"), None, None), P(("row", "col"), None, None), P(), P(), P())
    return jax.shard_map(shards, mesh=mesh, in_specs=in_specs, out_specs=out_specs, check_vma=False)
```

```python
import jax
import jax.numpy as jnp
from jax import lax
from jax.experimental import pallas as pl
from jax.experimental.pallas import tpu as pltpu
from jax.sharding import PartitionSpec as P

F32, BF16 = jnp.float32, jnp.bfloat16
BOTH = ("row", "col")


def transposed_dot(a, b):
    return lax.dot_general(a, b, (((0,), (0,)), ((), ())), preferred_element_type=F32)


def diagonal_kernel(place, mine, other, link, inverse_one, inverse_two, diag_one, cross, diag_two):
    low = place[0] == 0
    low, high = jnp.where(low, mine[...], other[...]), jnp.where(low, other[...], mine[...])
    sums = jnp.concatenate([low, high]).reshape(3, *link.shape)
    diag_one[...] = (inverse_one[...] + sums[0].astype(F32)).astype(BF16)
    step = jnp.dot(diag_one[...], link[...], preferred_element_type=F32)
    cross[...] = (sums[1].astype(F32) - step).astype(BF16)
    two = inverse_two[...] + sums[2].astype(F32) - transposed_dot(sums[1], link[...])
    diag_two[...] = (two - transposed_dot(link[...], cross[...])).astype(BF16)


def small_kernel(body, n_out, n_dots, tile, operands, scalars=0):
    memory = [pltpu.SMEM] * scalars + [pltpu.VMEM] * (len(operands) - scalars)
    return pl.pallas_call(
        body,
        out_shape=(jax.ShapeDtypeStruct((tile, tile), BF16),) * n_out,
        in_specs=[pl.BlockSpec(memory_space=space) for space in memory],
        out_specs=[pl.BlockSpec(memory_space=pltpu.VMEM)] * n_out,
        cost_estimate=pl.CostEstimate(
            flops=2 * n_dots * tile**3,
            bytes_accessed=4 * len(operands) * tile**2,
            transcendentals=0,
        ),
    )(*operands)


def after(array, *earlier):
    return lax.optimization_barrier((array, *earlier))[0]


def shards(
    ancestor,
    tile_mask,
    member_one,
    member_two,
    factor_one,
    factor_two,
    link_block,
    inverse_one,
    inverse_two,
):
    nrow, ncol = lax.axis_size("row"), lax.axis_size("col")
    row, col = lax.axis_index("row"), lax.axis_index("col")
    rows, cols, tile = ancestor.shape[0], ancestor.shape[1], ancestor.shape[-1]
    group = ncol // nrow
    bits, row_bits = ncol.bit_length() - 1, nrow.bit_length() - 1
    owner = col // group
    at = lambda r, c: r * ncol + c
    everyone = [(r, c) for r in range(nrow) for c in range(ncol)]

    def over_chips(piece, *earlier):
        have = piece
        for k in range(2, nrow, 2):
            perm = [(at(c // group, c), at((c // group + k) % nrow, c)) for c in range(ncol)]
            got = after(lax.ppermute(piece, BOTH, perm), *earlier)
            have = jnp.where((row - owner) % nrow == k, got, have)
        return have

    def over_cores(have):
        perm = [
            (at(2 * y + c // group % 2, c), at(2 * y + 1 - c // group % 2, c))
            for y in range(nrow // 2)
            for c in range(ncol)
        ]
        return jnp.where((row - owner) % 2 == 0, have, lax.ppermute(have, BOTH, perm))

    def swap(array, bit):
        return lax.ppermute(array, BOTH, [(at(r, c), at(r, c ^ (1 << bit))) for r, c in everyone])

    def swap_rows(array, bit):
        return lax.ppermute(array, BOTH, [(at(r, c), at(r ^ (1 << bit), c)) for r, c in everyone])

    def pick(array, bit, other):
        split = array.reshape(-1, 2, tile, tile)
        return lax.dynamic_slice_in_dim(split, (col >> bit & 1) ^ other, 1, 1)[:, 0].astype(F32)

    def first_swap(array, *earlier):
        away, keep = (pick(array, 0, other) for other in (1, 0))
        return keep, [swap(after(away.astype(BF16), *earlier), 0)]

    def next_swap(keep, arrived):
        bit = len(arrived)
        away, keep = (pick(keep, bit, other) + pick(arrived[-1], bit, other) for other in (1, 0))
        away = away.astype(BF16)
        arrived.append(swap(away, bit))
        return keep, away

    def part_of(array, start, size):
        return lax.dynamic_slice_in_dim(array, start, size, 0)

    def masked(marks, array):
        return jnp.where(marks.reshape(marks.shape + (1, 1)) > 0, array, jnp.zeros((), BF16))

    def products(marks, column):
        kept = masked(marks, ancestor)
        return jnp.einsum("ijab,jbc->iac", kept, column, preferred_element_type=F32).astype(BF16)

    def contraction(a, b):
        return jnp.einsum("sab,sac->bc", a, b, preferred_element_type=F32)

    flags_one, flags_two = (part_of(m, row * rows, rows) for m in (member_one, member_two))
    marks = [tile_mask * part_of(m, col * cols, cols)[None] for m in (member_one, member_two)]
    first, second = masked(flags_one, factor_one), masked(flags_two, factor_two)
    second_in_one = masked(flags_one, second)

    piece_one, piece_two = (part_of(f, col % group * cols, cols) for f in (factor_one, factor_two))
    piece_one, piece_two = after(piece_one), after(piece_two)
    have_one, have_two = over_chips(piece_one, *marks, flags_one, flags_two), over_chips(piece_two)
    all_one = products(marks[0], over_cores(have_one))
    keep_one, one = first_swap(all_one)
    all_two = products(marks[1], over_cores(after(have_two, all_one)))
    keep_two, two = first_swap(all_two)
    sums = contraction(first, all_one), contraction(all_one, second_in_one), contraction(second, all_two)
    for _ in range(1, bits):
        keep_one, _ = next_swap(keep_one, one)
        keep_two, last = next_swap(keep_two, two)

    sums = jnp.stack(sums)
    part = sums.reshape(-1, tile)
    for bit in range(row_bits):
        half = part.shape[0] // 2
        mine = row >> bit & 1
        got = swap_rows(lax.dynamic_slice_in_dim(part, (1 - mine) * half, half, 0).astype(BF16), bit)
        part = lax.dynamic_slice_in_dim(part, mine * half, half, 0) + got.astype(F32)
    part = part.astype(BF16)
    gates = {bits - 1: one[:1], 0: [two[0], *one[1:-1]]}
    for bit in reversed(range(bits)):
        got = swap(after(part, *gates.get(bit, ())), bit)
        part = (part.astype(F32) + got.astype(F32)).astype(BF16)
    one_last = after(one[-1], part)
    for bit in reversed(range(row_bits)):
        got = swap_rows(after(part, *((one_last, last) if bit == 0 else ())), bit)
        if bit:
            low = (row >> bit & 1) == 0
            part = jnp.concatenate([jnp.where(low, part, got), jnp.where(low, got, part)])

    member_one, member_two = (m[row * rows + col].astype(F32) for m in (member_one, member_two))
    column_one = (-member_one * (keep_one[0] + one_last[0].astype(F32))).astype(BF16)
    linked = jnp.dot(column_one, link_block, preferred_element_type=F32) + keep_two[0]
    column_two = (-member_two * (linked + two[-1][0].astype(F32))).astype(BF16)
    diag_one, cross_block, diag_two = small_kernel(
        diagonal_kernel,
        3,
        3,
        tile,
        ((row & 1)[None], part, after(got, column_two), link_block, inverse_one, inverse_two),
        1,
    )
    return (column_one[None], column_two[None], diag_one, cross_block, diag_two)


def solution(mesh):
    in_specs = (
        P("row", "col", None, None),
        P("row", "col"),
        P(),
        P(),
        P("row", None, None),
        P("row", None, None),
        P(),
        P(),
        P(),
    )
    out_specs = (P(("row", "col"), None, None), P(("row", "col"), None, None), P(), P(), P())
    return jax.shard_map(shards, mesh=mesh, in_specs=in_specs, out_specs=out_specs, check_vma=False)
```

```python
import jax
import jax.numpy as jnp
from jax import lax
from jax.experimental import pallas as pl
from jax.experimental.pallas import tpu as pltpu
from jax.sharding import PartitionSpec as P

F32, BF16 = jnp.float32, jnp.bfloat16
BOTH = ("row", "col")


def transposed_dot(a, b):
    return lax.dot_general(a, b, (((0,), (0,)), ((), ())), preferred_element_type=F32)


def diagonal_kernel(place, mine, other, link, inverse_one, inverse_two, diag_one, cross, diag_two):
    low = place[0] == 0
    low, high = jnp.where(low, mine[...], other[...]), jnp.where(low, other[...], mine[...])
    sums = jnp.concatenate([low, high]).reshape(3, *link.shape)
    diag_one[...] = (inverse_one[...] + sums[0].astype(F32)).astype(BF16)
    step = jnp.dot(diag_one[...], link[...], preferred_element_type=F32)
    cross[...] = (sums[1].astype(F32) - step).astype(BF16)
    two = inverse_two[...] + sums[2].astype(F32) - transposed_dot(sums[1], link[...])
    diag_two[...] = (two - transposed_dot(link[...], cross[...])).astype(BF16)


def small_kernel(body, n_out, n_dots, tile, operands, scalars=0):
    memory = [pltpu.SMEM] * scalars + [pltpu.VMEM] * (len(operands) - scalars)
    return pl.pallas_call(
        body,
        out_shape=(jax.ShapeDtypeStruct((tile, tile), BF16),) * n_out,
        in_specs=[pl.BlockSpec(memory_space=space) for space in memory],
        out_specs=[pl.BlockSpec(memory_space=pltpu.VMEM)] * n_out,
        cost_estimate=pl.CostEstimate(
            flops=2 * n_dots * tile**3,
            bytes_accessed=4 * len(operands) * tile**2,
            transcendentals=0,
        ),
    )(*operands)


def after(array, *earlier):
    return lax.optimization_barrier((array, *earlier))[0]


def shards(
    ancestor,
    tile_mask,
    member_one,
    member_two,
    factor_one,
    factor_two,
    link_block,
    inverse_one,
    inverse_two,
):
    nrow, ncol = lax.axis_size("row"), lax.axis_size("col")
    row, col = lax.axis_index("row"), lax.axis_index("col")
    rows, cols, tile = ancestor.shape[0], ancestor.shape[1], ancestor.shape[-1]
    group = ncol // nrow
    bits, row_bits = ncol.bit_length() - 1, nrow.bit_length() - 1
    owner = col // group
    at = lambda r, c: r * ncol + c
    everyone = [(r, c) for r in range(nrow) for c in range(ncol)]

    def over_chips(piece, *earlier):
        have = piece
        for k in range(2, nrow, 2):
            perm = [(at(c // group, c), at((c // group + k) % nrow, c)) for c in range(ncol)]
            got = after(lax.ppermute(piece, BOTH, perm), *earlier)
            have = jnp.where((row - owner) % nrow == k, got, have)
        return have

    def over_cores(have):
        perm = [
            (at(2 * y + c // group % 2, c), at(2 * y + 1 - c // group % 2, c))
            for y in range(nrow // 2)
            for c in range(ncol)
        ]
        return jnp.where((row - owner) % 2 == 0, have, lax.ppermute(have, BOTH, perm))

    def swap(array, bit):
        return lax.ppermute(array, BOTH, [(at(r, c), at(r, c ^ (1 << bit))) for r, c in everyone])

    def swap_rows(array, bit):
        return lax.ppermute(array, BOTH, [(at(r, c), at(r ^ (1 << bit), c)) for r, c in everyone])

    def pick(array, bit, other):
        split = array.reshape(-1, 2, tile, tile)
        return lax.dynamic_slice_in_dim(split, (col >> bit & 1) ^ other, 1, 1)[:, 0].astype(F32)

    def first_swap(array, *earlier):
        away, keep = (pick(array, 0, other) for other in (1, 0))
        return keep, [swap(after(away.astype(BF16), *earlier), 0)]

    def next_swap(keep, arrived):
        bit = len(arrived)
        away, keep = (pick(keep, bit, other) + pick(arrived[-1], bit, other) for other in (1, 0))
        arrived.append(swap(away.astype(BF16), bit))
        return keep

    def part_of(array, start, size):
        return lax.dynamic_slice_in_dim(array, start, size, 0)

    def masked(marks, array):
        return jnp.where(marks.reshape(marks.shape + (1, 1)) > 0, array, jnp.zeros((), BF16))

    def products(marks, column):
        kept = masked(marks, ancestor)
        return jnp.einsum("ijab,jbc->iac", kept, column, preferred_element_type=F32).astype(BF16)

    def contraction(a, b):
        return jnp.einsum("sab,sac->bc", a, b, preferred_element_type=F32)

    flags_one, flags_two = (part_of(m, row * rows, rows) for m in (member_one, member_two))
    marks = [tile_mask * part_of(m, col * cols, cols)[None] for m in (member_one, member_two)]
    first, second = masked(flags_one, factor_one), masked(flags_two, factor_two)
    second_in_one = masked(flags_one, second)

    piece_one, piece_two = (part_of(f, col % group * cols, cols) for f in (factor_one, factor_two))
    piece_one, piece_two = after(piece_one), after(piece_two)
    have_one, have_two = over_chips(piece_one, *marks, flags_one, flags_two), over_chips(piece_two)
    all_one = products(marks[0], over_cores(have_one))
    keep_one, one = first_swap(all_one)
    all_two = products(marks[1], over_cores(after(have_two, all_one)))
    keep_two, two = first_swap(all_two, one[0])
    sums = contraction(first, all_one), contraction(all_one, second_in_one), contraction(second, all_two)
    for _ in range(1, bits):
        keep_one = next_swap(keep_one, one)
        keep_two = next_swap(keep_two, two)

    sums = jnp.stack(sums)
    part = sums.reshape(-1, tile)
    for bit in range(row_bits):
        half = part.shape[0] // 2
        mine = row >> bit & 1
        got = swap_rows(lax.dynamic_slice_in_dim(part, (1 - mine) * half, half, 0).astype(BF16), bit)
        part = lax.dynamic_slice_in_dim(part, mine * half, half, 0) + got.astype(F32)
    part = part.astype(BF16)
    gates = [one[0], two[0], *one[1:]]
    for bit, gate in zip(reversed(range(bits)), gates):
        got = swap(after(part, gate), bit)
        part = (part.astype(F32) + got.astype(F32)).astype(BF16)
    for bit in reversed(range(row_bits)):
        got = swap_rows(after(part, *((two[-2], one[-1]) if bit == 0 else ())), bit)
        if bit:
            low = (row >> bit & 1) == 0
            part = jnp.concatenate([jnp.where(low, part, got), jnp.where(low, got, part)])

    member_one, member_two = (m[row * rows + col].astype(F32) for m in (member_one, member_two))
    column_one = (-member_one * (keep_one[0] + after(one[-1], got)[0].astype(F32))).astype(BF16)
    linked = jnp.dot(column_one, link_block, preferred_element_type=F32) + keep_two[0]
    column_two = (-member_two * (linked + two[-1][0].astype(F32))).astype(BF16)
    diag_one, cross_block, diag_two = small_kernel(
        diagonal_kernel,
        3,
        3,
        tile,
        ((row & 1)[None], part, after(got, column_two), link_block, inverse_one, inverse_two),
        1,
    )
    return (column_one[None], column_two[None], diag_one, cross_block, diag_two)


def solution(mesh):
    in_specs = (
        P("row", "col", None, None),
        P("row", "col"),
        P(),
        P(),
        P("row", None, None),
        P("row", None, None),
        P(),
        P(),
        P(),
    )
    out_specs = (P(("row", "col"), None, None), P(("row", "col"), None, None), P(), P(), P())
    return jax.shard_map(shards, mesh=mesh, in_specs=in_specs, out_specs=out_specs, check_vma=False)
```

```python
import jax
import jax.numpy as jnp
from jax import lax
from jax.experimental import pallas as pl
from jax.experimental.pallas import tpu as pltpu
from jax.sharding import PartitionSpec as P

F32, BF16 = jnp.float32, jnp.bfloat16
BOTH = ("row", "col")


def transposed_dot(a, b):
    return lax.dot_general(a, b, (((0,), (0,)), ((), ())), preferred_element_type=F32)


def diagonal_kernel(place, mine, other, link, inverse_one, inverse_two, diag_one, cross, diag_two):
    low = place[0] == 0
    low, high = jnp.where(low, mine[...], other[...]), jnp.where(low, other[...], mine[...])
    sums = jnp.concatenate([low, high]).reshape(3, *link.shape)
    diag_one[...] = (inverse_one[...] + sums[0].astype(F32)).astype(BF16)
    step = jnp.dot(diag_one[...], link[...], preferred_element_type=F32)
    cross[...] = (sums[1].astype(F32) - step).astype(BF16)
    two = inverse_two[...] + sums[2].astype(F32) - transposed_dot(sums[1], link[...])
    diag_two[...] = (two - transposed_dot(link[...], cross[...])).astype(BF16)


def small_kernel(body, n_out, n_dots, tile, operands, scalars=0):
    memory = [pltpu.SMEM] * scalars + [pltpu.VMEM] * (len(operands) - scalars)
    return pl.pallas_call(
        body,
        out_shape=(jax.ShapeDtypeStruct((tile, tile), BF16),) * n_out,
        in_specs=[pl.BlockSpec(memory_space=space) for space in memory],
        out_specs=[pl.BlockSpec(memory_space=pltpu.VMEM)] * n_out,
        cost_estimate=pl.CostEstimate(
            flops=2 * n_dots * tile**3,
            bytes_accessed=4 * len(operands) * tile**2,
            transcendentals=0,
        ),
    )(*operands)


def after(array, *earlier):
    return lax.optimization_barrier((array, *earlier))[0]


def shards(
    ancestor,
    tile_mask,
    member_one,
    member_two,
    factor_one,
    factor_two,
    link_block,
    inverse_one,
    inverse_two,
):
    nrow, ncol = lax.axis_size("row"), lax.axis_size("col")
    row, col = lax.axis_index("row"), lax.axis_index("col")
    rows, cols, tile = ancestor.shape[0], ancestor.shape[1], ancestor.shape[-1]
    group = ncol // nrow
    bits, row_bits = ncol.bit_length() - 1, nrow.bit_length() - 1
    owner = col // group
    at = lambda r, c: r * ncol + c
    everyone = [(r, c) for r in range(nrow) for c in range(ncol)]

    def over_chips(piece, *earlier):
        have = piece
        for k in range(2, nrow, 2):
            perm = [(at(c // group, c), at((c // group + k) % nrow, c)) for c in range(ncol)]
            got = after(lax.ppermute(piece, BOTH, perm), *earlier)
            have = jnp.where((row - owner) % nrow == k, got, have)
        return have

    def over_cores(have):
        perm = [
            (at(2 * y + c // group % 2, c), at(2 * y + 1 - c // group % 2, c))
            for y in range(nrow // 2)
            for c in range(ncol)
        ]
        return jnp.where((row - owner) % 2 == 0, have, lax.ppermute(have, BOTH, perm))

    def swap(array, bit):
        return lax.ppermute(array, BOTH, [(at(r, c), at(r, c ^ (1 << bit))) for r, c in everyone])

    def swap_rows(array, bit):
        return lax.ppermute(array, BOTH, [(at(r, c), at(r ^ (1 << bit), c)) for r, c in everyone])

    def pick(array, bit, other):
        split = array.reshape(-1, 2, tile, tile)
        return lax.dynamic_slice_in_dim(split, (col >> bit & 1) ^ other, 1, 1)[:, 0].astype(F32)

    def first_swap(array, *earlier):
        away, keep = (pick(array, 0, other) for other in (1, 0))
        return keep, [swap(after(away.astype(BF16), *earlier), 0)]

    def next_swap(keep, arrived):
        bit = len(arrived)
        away, keep = (pick(keep, bit, other) + pick(arrived[-1], bit, other) for other in (1, 0))
        arrived.append(swap(away.astype(BF16), bit))
        return keep

    def part_of(array, start, size):
        return lax.dynamic_slice_in_dim(array, start, size, 0)

    def masked(marks, array):
        return jnp.where(marks.reshape(marks.shape + (1, 1)) > 0, array, jnp.zeros((), BF16))

    def products(marks, column):
        kept = masked(marks, ancestor)
        return jnp.einsum("ijab,jbc->iac", kept, column, preferred_element_type=F32).astype(BF16)

    def contraction(a, b):
        return jnp.einsum("sab,sac->bc", a, b, preferred_element_type=F32)

    flags_one, flags_two = (part_of(m, row * rows, rows) for m in (member_one, member_two))
    marks = [tile_mask * part_of(m, col * cols, cols)[None] for m in (member_one, member_two)]
    first, second = masked(flags_one, factor_one), masked(flags_two, factor_two)
    second_in_one = masked(flags_one, second)

    piece_one, piece_two = (part_of(f, col % group * cols, cols) for f in (factor_one, factor_two))
    piece_one, piece_two = after(piece_one), after(piece_two)
    have_one, have_two = over_chips(piece_one, *marks, flags_one, flags_two), over_chips(piece_two)
    all_one = products(marks[0], over_cores(have_one))
    keep_one, one = first_swap(all_one)
    all_two = products(marks[1], over_cores(after(have_two, all_one)))
    keep_two, two = first_swap(all_two, one[0])
    sums = contraction(first, all_one), contraction(all_one, second_in_one), contraction(second, all_two)
    for _ in range(1, bits):
        keep_one = next_swap(keep_one, one)
        keep_two = next_swap(keep_two, two)

    sums = jnp.stack(sums)
    part = sums.reshape(-1, tile)
    for bit in range(row_bits):
        half = part.shape[0] // 2
        mine = row >> bit & 1
        got = swap_rows(lax.dynamic_slice_in_dim(part, (1 - mine) * half, half, 0).astype(BF16), bit)
        part = lax.dynamic_slice_in_dim(part, mine * half, half, 0) + got.astype(F32)
    part = part.astype(BF16)
    gates = [one[0], two[0], *one[1:]]
    for bit, gate in zip(reversed(range(bits)), gates):
        got = swap(after(part, gate), bit)
        part = (part.astype(F32) + got.astype(F32)).astype(BF16)
    for bit in reversed(range(row_bits)):
        got = swap_rows(after(part, one[-1] if bit == 0 else two[-2]), bit)
        if bit:
            low = (row >> bit & 1) == 0
            part = jnp.concatenate([jnp.where(low, part, got), jnp.where(low, got, part)])

    member_one, member_two = (m[row * rows + col].astype(F32) for m in (member_one, member_two))
    column_one = (-member_one * (keep_one[0] + after(one[-1], part)[0].astype(F32))).astype(BF16)
    linked = jnp.dot(column_one, link_block, preferred_element_type=F32) + keep_two[0]
    column_two = (-member_two * (linked + two[-1][0].astype(F32))).astype(BF16)
    diag_one, cross_block, diag_two = small_kernel(
        diagonal_kernel,
        3,
        3,
        tile,
        ((row & 1)[None], part, after(got, column_two), link_block, inverse_one, inverse_two),
        1,
    )
    return (column_one[None], column_two[None], diag_one, cross_block, diag_two)


def solution(mesh):
    in_specs = (
        P("row", "col", None, None),
        P("row", "col"),
        P(),
        P(),
        P("row", None, None),
        P("row", None, None),
        P(),
        P(),
        P(),
    )
    out_specs = (P(("row", "col"), None, None), P(("row", "col"), None, None), P(), P(), P())
    return jax.shard_map(shards, mesh=mesh, in_specs=in_specs, out_specs=out_specs, check_vma=False)
```

```python
import jax
import jax.numpy as jnp
from jax import lax
from jax.experimental import pallas as pl
from jax.experimental.pallas import tpu as pltpu
from jax.sharding import PartitionSpec as P

F32, BF16 = jnp.float32, jnp.bfloat16
BOTH = ("row", "col")


def transposed_dot(a, b):
    return lax.dot_general(a, b, (((0,), (0,)), ((), ())), preferred_element_type=F32)


def diagonal_kernel(place, mine, other, link, inverse_one, inverse_two, diag_one, cross, diag_two):
    low = place[0] == 0
    low, high = jnp.where(low, mine[...], other[...]), jnp.where(low, other[...], mine[...])
    sums = jnp.concatenate([low, high]).reshape(3, *link.shape)
    diag_one[...] = (inverse_one[...] + sums[0].astype(F32)).astype(BF16)
    step = jnp.dot(diag_one[...], link[...], preferred_element_type=F32)
    cross[...] = (sums[1].astype(F32) - step).astype(BF16)
    two = inverse_two[...] + sums[2].astype(F32) - transposed_dot(sums[1], link[...])
    diag_two[...] = (two - transposed_dot(link[...], cross[...])).astype(BF16)


def small_kernel(body, n_out, n_dots, tile, operands, scalars=0):
    memory = [pltpu.SMEM] * scalars + [pltpu.VMEM] * (len(operands) - scalars)
    return pl.pallas_call(
        body,
        out_shape=(jax.ShapeDtypeStruct((tile, tile), BF16),) * n_out,
        in_specs=[pl.BlockSpec(memory_space=space) for space in memory],
        out_specs=[pl.BlockSpec(memory_space=pltpu.VMEM)] * n_out,
        cost_estimate=pl.CostEstimate(
            flops=2 * n_dots * tile**3,
            bytes_accessed=4 * len(operands) * tile**2,
            transcendentals=0,
        ),
    )(*operands)


def after(array, *earlier):
    return lax.optimization_barrier((array, *earlier))[0]


def shards(
    ancestor,
    tile_mask,
    member_one,
    member_two,
    factor_one,
    factor_two,
    link_block,
    inverse_one,
    inverse_two,
):
    nrow, ncol = lax.axis_size("row"), lax.axis_size("col")
    row, col = lax.axis_index("row"), lax.axis_index("col")
    rows, cols, tile = ancestor.shape[0], ancestor.shape[1], ancestor.shape[-1]
    group = ncol // nrow
    bits, row_bits = ncol.bit_length() - 1, nrow.bit_length() - 1
    owner = col // group
    at = lambda r, c: r * ncol + c
    everyone = [(r, c) for r in range(nrow) for c in range(ncol)]

    def over_chips(piece, *earlier):
        have = piece
        for k in range(2, nrow, 2):
            perm = [(at(c // group, c), at((c // group + k) % nrow, c)) for c in range(ncol)]
            got = after(lax.ppermute(piece, BOTH, perm), *earlier)
            have = jnp.where((row - owner) % nrow == k, got, have)
        return have

    def over_cores(have):
        perm = [
            (at(2 * y + c // group % 2, c), at(2 * y + 1 - c // group % 2, c))
            for y in range(nrow // 2)
            for c in range(ncol)
        ]
        return jnp.where((row - owner) % 2 == 0, have, lax.ppermute(have, BOTH, perm))

    def swap(array, bit):
        return lax.ppermute(array, BOTH, [(at(r, c), at(r, c ^ (1 << bit))) for r, c in everyone])

    def swap_rows(array, bit):
        return lax.ppermute(array, BOTH, [(at(r, c), at(r ^ (1 << bit), c)) for r, c in everyone])

    def pick(array, bit, other):
        split = array.reshape(-1, 2, tile, tile)
        return lax.dynamic_slice_in_dim(split, (col >> bit & 1) ^ other, 1, 1)[:, 0].astype(F32)

    def first_swap(array, *earlier):
        away, keep = (pick(array, 0, other) for other in (1, 0))
        return keep, [swap(after(away.astype(BF16), *earlier), 0)]

    def next_swap(keep, arrived):
        bit = len(arrived)
        away, keep = (pick(keep, bit, other) + pick(arrived[-1], bit, other) for other in (1, 0))
        arrived.append(swap(away.astype(BF16), bit))
        return keep

    def part_of(array, start, size):
        return lax.dynamic_slice_in_dim(array, start, size, 0)

    def masked(marks, array):
        return jnp.where(marks.reshape(marks.shape + (1, 1)) > 0, array, jnp.zeros((), BF16))

    def products(marks, column):
        kept = masked(marks, ancestor)
        return jnp.einsum("ijab,jbc->iac", kept, column, preferred_element_type=F32).astype(BF16)

    def contraction(a, b):
        return jnp.einsum("sab,sac->bc", a, b, preferred_element_type=F32)

    flags_one, flags_two = (part_of(m, row * rows, rows) for m in (member_one, member_two))
    marks = [tile_mask * part_of(m, col * cols, cols)[None] for m in (member_one, member_two)]
    first, second = masked(flags_one, factor_one), masked(flags_two, factor_two)
    second_in_one = masked(flags_one, second)

    piece_one, piece_two = (part_of(f, col % group * cols, cols) for f in (factor_one, factor_two))
    piece_one, piece_two = after(piece_one), after(piece_two)
    have_one, have_two = over_chips(piece_one, *marks, flags_one, flags_two), over_chips(piece_two)
    all_one = products(marks[0], over_cores(have_one))
    keep_one, one = first_swap(all_one)
    all_two = products(marks[1], over_cores(after(have_two, all_one)))
    keep_two, two = first_swap(all_two, one[0])
    all_one = after(all_one, all_two)
    sums = contraction(first, all_one), contraction(all_one, second_in_one), contraction(second, all_two)
    for _ in range(1, bits):
        keep_one = next_swap(keep_one, one)
        keep_two = next_swap(keep_two, two)

    sums = jnp.stack(sums)
    part = sums.reshape(-1, tile)
    for bit in range(row_bits):
        half = part.shape[0] // 2
        mine = row >> bit & 1
        got = swap_rows(lax.dynamic_slice_in_dim(part, (1 - mine) * half, half, 0).astype(BF16), bit)
        part = lax.dynamic_slice_in_dim(part, mine * half, half, 0) + got.astype(F32)
    part = part.astype(BF16)
    gates = [one[0], two[0], *one[1:]]
    for bit, gate in zip(reversed(range(bits)), gates):
        got = swap(after(part, gate), bit)
        part = (part.astype(F32) + got.astype(F32)).astype(BF16)
    for bit in reversed(range(row_bits)):
        got = swap_rows(after(part, one[-1] if bit == 0 else two[-2]), bit)
        if bit:
            low = (row >> bit & 1) == 0
            part = jnp.concatenate([jnp.where(low, part, got), jnp.where(low, got, part)])

    diag_one, cross_block, diag_two = small_kernel(
        diagonal_kernel,
        3,
        3,
        tile,
        ((row & 1)[None], part, got, link_block, inverse_one, inverse_two),
        1,
    )
    member_one, member_two = (m[row * rows + col].astype(F32) for m in (member_one, member_two))
    column_one = (-member_one * (keep_one[0] + one[-1][0].astype(F32))).astype(BF16)
    linked = jnp.dot(column_one, link_block, preferred_element_type=F32) + keep_two[0]
    column_two = (-member_two * (linked + after(two[-1], diag_two)[0].astype(F32))).astype(BF16)
    return (column_one[None], column_two[None], diag_one, cross_block, diag_two)


def solution(mesh):
    in_specs = (
        P("row", "col", None, None),
        P("row", "col"),
        P(),
        P(),
        P("row", None, None),
        P("row", None, None),
        P(),
        P(),
        P(),
    )
    out_specs = (P(("row", "col"), None, None), P(("row", "col"), None, None), P(), P(), P())
    return jax.shard_map(shards, mesh=mesh, in_specs=in_specs, out_specs=out_specs, check_vma=False)
```
